32 devices in a mesh: groups: 2 (over x), mp: 8 (over z, y), sub: 2 (over core).
Axes of the slice: x: 2, y: 2, z: 4, core: 2. Of those that a mesh axis runs over, the one named last changes fastest.
Arguments:
- tokens: bfloat16 [1024, 8192], P(('groups', 'mp'), 'sub'), parts along dimension 0, may hold values from -6 to 6
- gate_matrix: bfloat16 [8192, 28672], P('sub', 'mp'), may hold values from -0.0625 to 0.0625
- adapter_down_panels: bfloat16 [8, 8192, 64], P('mp', 'sub'), may hold values from -0.0625 to 0.0625
- adapter_up_panels: bfloat16 [8, 64, 28672], P('mp'), may hold values from -0.75 to 0.75
- request_adapter_index: int32 [512, 1], P('groups'), parts along dimension 0, may hold values from 0 to 7; in each aligned block of 256 rows (0 to 255, 256 to 511, ...) at most 64 rows name the same one
- adapter_store_row: int32 [8], replicated, may hold values from 0 to 7, each once
Outputs:
- gated: bfloat16 [1024, 28672], P(('groups', 'sub'), 'mp'), parts along dimension 0
The draws below stay inside these ranges and needn't reach their ends.
There are 2 independent parts, one for each index of `groups`. The reference program is written for one: setup_inputs(seed, part) draws one part's arguments, and reference() takes and returns one part's arrays. A program takes and returns all parts, laid end to end along the dimension named above; an argument that names none is the same for every part. Nothing has to cross between parts.
Inputs may be any that keep to these rules, and one draw needn't show every extreme that they name: `request_adapter_index`: in each part no adapter serves more than 64 requests, and some adapter serves exactly 64. `adapter_store_row`: each store row once.
All inputs are finite; a program needn't handle non-finite values.
Results may differ from the reference program's by a relative error of at most 0.0039.
Values may be sent and summed in bfloat16 or wider, within the bound.
No kernel may reach another device: no remote copies, remote signals or barrier semaphores. Data moves between devices by JAX's collectives and lax.ppermute only.
A program may use at most 192 MiB of HBM per device.

```python
import math
import jax
import jax.numpy as jnp
import numpy as np
from jax import lax

MODEL_WIDTH = 8192
HIDDEN_UNITS = 28672
ADAPTER_RANK = 64
TOK_DEV = 64
TOKENS = 512
REQUESTS = 256
ADAPTER_COUNT = 8


def block_levels(stream_key, dims, split, smallest, top_value):
    factor_of, own = 1.0, jax.random.fold_in(stream_key, 6)
    for axis_at, shards_of in split:
        draws = jnp.exp(jax.random.uniform(jax.random.fold_in(own, axis_at), (shards_of,), jnp.float32, smallest / len(split), top_value / len(split)))
        factor_of = factor_of * jnp.repeat(draws, dims[axis_at] // shards_of).reshape([-1 if axis == axis_at else 1 for axis in range(len(dims))])
    return factor_of


def deal_out(stream_key, own, number, rows, number_of, top, reach, slope):
    order = jax.random.permutation(stream_key, number_of)
    heavy_load, usual = portions_of(number_of, rows * top, reach, slope, True), portions_of(number_of, rows * top, reach, slope, False)
    places = jnp.arange(number_of)

    def named(tallies, turn):
        used = int((tallies > 0).sum())
        fixed = max(1, used // 4)
        passed = fixed + (places - fixed + turn * (used - fixed)) % max(1, number_of - fixed)
        return jnp.zeros((number_of,), jnp.int32).at[order[jnp.where(places < fixed, places, passed)]].set(jnp.asarray(tallies, jnp.int32))

    tallies = jnp.where(number % 4 == 0, named(heavy_load, number // 4), named(usual, number - number // 4 - 1))
    mixed = jax.random.permutation(jax.random.fold_in(own, 3), number_of)
    giver, taker = mixed[0:number_of // 2 * 2:2], mixed[1:number_of // 2 * 2:2]
    slack = jnp.minimum(tallies[giver] - 1, reach - tallies[taker]) // 2
    slack = jnp.where((giver == order[0]) | (taker == order[0]) | (tallies[taker] == 0), 0, jnp.maximum(slack, 0))
    passed = jax.random.randint(jax.random.fold_in(own, 4), (number_of // 2,), 0, 1 << 20) % (slack + 1)
    tallies = tallies.at[giver].add(-passed).at[taker].add(passed)
    items = jnp.searchsorted(jnp.cumsum(tallies), jnp.arange(rows * top), side="right").astype(jnp.int32)
    grid = items.reshape(top, rows).T
    grid = grid[jax.random.permutation(jax.random.fold_in(own, 1), rows)]
    turn = jax.random.randint(jax.random.fold_in(own, 2), (rows, 1), 0, top)
    return jnp.take_along_axis(grid, (jnp.arange(top)[None, :] + turn) % top, axis=1)


def portions_of(number_of, total, reach, slope, full):
    portions = [(1 << 20) // math.isqrt(rank ** slope) + 1 for rank in range(1, number_of + 1)]
    largest = reach if full else min(reach, max(-(-total // number_of), total * portions[0] // sum(portions)))
    least = 1 if total - largest >= number_of - 1 else 0
    holding, surplus = [largest] + [least] * (number_of - 1), total - largest - least * (number_of - 1)
    while surplus > 0:
        free = [i for i in range(1, number_of) if holding[i] < largest] or [i for i in range(1, number_of) if holding[i] < reach]
        pool, left = sum([portions[i] for i in free]), surplus
        for i in free:
            extra = min(reach - holding[i], max(1, left * portions[i] // pool), surplus)
            holding[i] = holding[i] + extra
            surplus = surplus - extra
    return np.array(holding)


def normal_values(rng, extent, spread, bound, pieces=(), kind=jnp.bfloat16):
    level = block_levels(rng, extent, pieces, -0.22, 0.18) if pieces else 1.0
    array = jax.random.normal(rng, extent, jnp.float32) * spread * level
    return jnp.minimum(jnp.maximum(array, -bound), bound).astype(kind)


def setup_inputs(seed: int = 0, part: int = 0) -> dict:
    keys = jax.random.split(jax.random.key(seed), 7)
    part_keys = jax.random.split(jax.random.fold_in(keys[6], part), 7)
    tokens = normal_values(part_keys[0], (TOKENS, MODEL_WIDTH), 1.0, 6.0, ((0, 8), (1, 2)))
    gate_matrix = normal_values(keys[1], (MODEL_WIDTH, HIDDEN_UNITS), MODEL_WIDTH ** -0.5, 0.0625, ((0, 2), (1, 8)))
    adapter_down_panels = normal_values(keys[2], (ADAPTER_COUNT, MODEL_WIDTH, ADAPTER_RANK), MODEL_WIDTH ** -0.5, 0.0625, ((0, 8), (1, 2)))
    adapter_up_panels = normal_values(keys[3], (ADAPTER_COUNT, ADAPTER_RANK, HIDDEN_UNITS), ADAPTER_RANK ** -0.5, 0.75, ((0, 8),))
    request_adapter_index_keys = jax.random.split(jax.random.fold_in(part_keys[4], 1), REQUESTS // REQUESTS)
    request_adapter_index_turns = jax.random.permutation(jax.random.fold_in(part_keys[4], 3), REQUESTS // REQUESTS)
    request_adapter_index = jax.vmap(lambda own, number: deal_out(jax.random.fold_in(part_keys[4], 2), own, number, REQUESTS, ADAPTER_COUNT, 1, TOK_DEV, 1))(request_adapter_index_keys, request_adapter_index_turns).reshape((REQUESTS, 1))
    adapter_store_row = jax.random.permutation(keys[5], ADAPTER_COUNT).astype(jnp.int32)
    return dict(tokens=tokens, gate_matrix=gate_matrix, adapter_down_panels=adapter_down_panels, adapter_up_panels=adapter_up_panels, request_adapter_index=request_adapter_index, adapter_store_row=adapter_store_row)


def reference(tokens, gate_matrix, adapter_down_panels, adapter_up_panels, request_adapter_index, adapter_store_row):
    per_token = jnp.repeat(request_adapter_index[:, 0], 2, total_repeat_length=TOKENS)
    store_row = adapter_store_row[per_token].astype(jnp.int32)
    base = jnp.dot(tokens, gate_matrix, preferred_element_type=jnp.float32)

    def down_step(carry, chosen_row):
        selector = (store_row == chosen_row).astype(jnp.float32)[:, None]
        gate_output = jnp.dot(tokens, adapter_down_panels[chosen_row], preferred_element_type=jnp.float32)
        return carry + selector * gate_output, None

    low, _ = lax.scan(down_step, jnp.zeros((TOKENS, ADAPTER_RANK), jnp.float32), jnp.arange(ADAPTER_COUNT, dtype=jnp.int32))
    low_rank_batch = low.astype(jnp.bfloat16)

    def up_step(carry, chosen_row):
        selector = (store_row == chosen_row).astype(jnp.float32)[:, None]
        gate_output = jnp.dot(low_rank_batch, adapter_up_panels[chosen_row], preferred_element_type=jnp.float32)
        return carry + selector * gate_output, None

    delta, _ = lax.scan(up_step, jnp.zeros((TOKENS, HIDDEN_UNITS), jnp.float32), jnp.arange(ADAPTER_COUNT, dtype=jnp.int32))
    return (base + delta).astype(jnp.bfloat16)
```

```python
import jax
import jax.numpy as jnp
from jax import lax
from jax.experimental import pallas as pl
from jax.experimental.pallas import tpu as pltpu
from jax.sharding import PartitionSpec as P

F32 = jnp.float32
BF16 = jnp.bfloat16
ANY = pl.BlockSpec(memory_space=pl.ANY)
VMEM = pl.BlockSpec(memory_space=pltpu.VMEM)


def params(mib):
    return pltpu.CompilerParams(vmem_limit_bytes=mib << 20)


def split_panels(up, count, groups):
    rank, hidden = up.shape[1], up.shape[2]
    quarter, width = rank // 4, hidden // count

    def kernel(up_ref, out_ref, sem):
        which = 2 * lax.rem(lax.axis_index("groups"), 2) + lax.axis_index("sub")
        rows = pl.ds(pl.multiple_of(which * quarter, quarter), quarter)
        copies = [
            pltpu.make_async_copy(
                up_ref.at[0, rows, pl.ds(d * width, width)], out_ref.at[d], sem.at[d]
            )
            for d in range(count)
        ]
        for copy in copies:
            copy.start()
        for copy in copies:
            copy.wait()

    return pl.pallas_call(
        kernel,
        in_specs=[ANY],
        out_specs=ANY,
        out_shape=jax.ShapeDtypeStruct((count, quarter, width), BF16),
        scratch_shapes=[pltpu.SemaphoreType.DMA((count,))],
        name="split_panels",
        cost_estimate=pl.CostEstimate(
            flops=0, bytes_accessed=4 * count * quarter * width, transcendentals=0
        ),
    )(up)


def place(step, levels):
    index = lax.axis_index("mp")
    origin = lax.rem(index // 2 - step + levels, levels)
    keeps_first = (origin // (levels // 2)) == lax.axis_index("sub")
    return keeps_first, lax.rem(index, 2)


def load_rows(chunks, rows_ref, sem, step, levels):
    keeps_first, y = place(step, levels)
    shard = chunks[0].shape[0]
    first = jnp.where(keeps_first, 0, 2 * shard)
    starts = [
        first + y * shard,
        first + (1 - y) * shard,
        2 * shard - first + y * shard,
        2 * shard - first + (1 - y) * shard,
    ]
    copies = [
        pltpu.make_async_copy(
            chunk, rows_ref.at[pl.ds(pl.multiple_of(start, shard), shard)], sem.at[i]
        )
        for i, (chunk, start) in enumerate(zip(chunks, starts))
    ]
    for copy in copies:
        copy.start()
    for copy in copies:
        copy.wait()


def base_pair(chunks, gate, step, levels):
    shard, depth = chunks[0].shape
    width = gate.shape[1]
    tile = 512 if width % 512 == 0 else 256
    half = 2 * shard

    def kernel(c0, c1, c2, c3, gate_ref, keep_ref, send_ref, rows_ref, sem):
        @pl.when(pl.program_id(0) == 0)
        def _():
            load_rows((c0, c1, c2, c3), rows_ref, sem, step, levels)

        columns = pl.ds(pl.multiple_of(pl.program_id(0) * tile, tile), tile)
        total = jnp.dot(rows_ref[...], gate_ref[:, columns], preferred_element_type=F32)
        keep_ref[...] = total[:half]
        send_ref[...] = total[half:].astype(BF16)

    return pl.pallas_call(
        kernel,
        grid=(width // tile,),
        in_specs=[ANY] * 4 + [VMEM],
        out_specs=[pl.BlockSpec((half, tile), lambda i: (0, i))] * 2,
        out_shape=[
            jax.ShapeDtypeStruct((half, width), F32),
            jax.ShapeDtypeStruct((half, width), BF16),
        ],
        scratch_shapes=[
            pltpu.VMEM((2 * half, depth), BF16),
            pltpu.SemaphoreType.DMA((4,)),
        ],
        compiler_params=params(12),
        name="base_pair",
        cost_estimate=pl.CostEstimate(
            flops=4 * half * depth * width,
            bytes_accessed=4 * half * depth + 6 * half * width,
            transcendentals=0,
        ),
    )(*chunks, gate)


def low_pair(chunks, down, step, levels):
    shard, depth = chunks[0].shape
    rank = down.shape[2]
    half = 2 * shard

    def kernel(c0, c1, c2, c3, down_ref, keep_ref, send_ref, rows_ref, sem):
        load_rows((c0, c1, c2, c3), rows_ref, sem, step, levels)
        total = jnp.dot(rows_ref[...], down_ref[0], preferred_element_type=F32)
        keep_ref[...] = total[:half]
        send_ref[...] = total[half:]

    return pl.pallas_call(
        kernel,
        in_specs=[ANY] * 4 + [VMEM],
        out_specs=[VMEM] * 2,
        out_shape=[jax.ShapeDtypeStruct((half, rank), F32)] * 2,
        scratch_shapes=[
            pltpu.VMEM((2 * half, depth), BF16),
            pltpu.SemaphoreType.DMA((4,)),
        ],
        compiler_params=params(12),
        name="low_pair",
        cost_estimate=pl.CostEstimate(
            flops=4 * half * depth * rank,
            bytes_accessed=4 * half * depth + 2 * depth * rank,
            transcendentals=0,
        ),
    )(*chunks, down)


def low_own(keeps, receives, store_row, levels):
    half, rank = keeps[0].shape
    pairs = levels // 2

    def kernel(*refs):
        row_ref, out_ref = refs[-2], refs[-1]
        index = lax.axis_index("mp")
        for k in range(pairs):
            at = lax.rem(index // 2 - k + levels, pairs)
            rows = pl.ds(pl.multiple_of(at * half, half), half)
            total = refs[k][...] + refs[pairs + k][...]
            total = jnp.where(row_ref[rows, :] == index, total, 0.0)
            out_ref[rows, :] = total.astype(BF16)

    return pl.pallas_call(
        kernel,
        in_specs=[VMEM] * (2 * pairs + 1),
        out_specs=VMEM,
        out_shape=jax.ShapeDtypeStruct((pairs * half, rank), BF16),
        name="low_own",
        cost_estimate=pl.CostEstimate(
            flops=pairs * half * rank, bytes_accessed=10 * pairs * half * rank, transcendentals=0
        ),
    )(*keeps, *receives, store_row)


def finish(keeps, receives, low, store_row, panels, levels):
    half, width = keeps[0].shape
    pairs = levels // 2
    total_rows, rank = low.shape
    count, quarter, _ = panels[0].shape
    tile = 512 if width % 512 == 0 else 256

    def kernel(*refs):
        keep_refs, receive_refs = refs[:pairs], refs[pairs : 2 * pairs]
        low_ref, row_ref = refs[2 * pairs : 2 * pairs + 2]
        panel_refs = refs[2 * pairs + 2 : 2 * pairs + 6]
        out_ref, spread_ref = refs[-2:]

        @pl.when(pl.program_id(0) == 0)
        def _():
            group, core = lax.rem(lax.axis_index("groups"), 2), lax.axis_index("sub")
            at = lax.broadcasted_iota(jnp.int32, (rank, count * quarter), 0)
            to = lax.broadcasted_iota(jnp.int32, (rank, count * quarter), 1)
            mine = (
                lax.broadcasted_iota(jnp.int32, (total_rows, count * quarter), 1) // quarter
                == row_ref[...]
            )
            for i, (own_group, own_core) in enumerate(
                ((True, True), (False, True), (True, False), (False, False))
            ):
                which = 2 * (group if own_group else 1 - group) + (core if own_core else 1 - core)
                picks = (at == which * quarter + lax.rem(to, quarter)).astype(BF16)
                spread = jnp.dot(low_ref[...], picks, preferred_element_type=F32)
                spread_ref[i] = jnp.where(mine, spread, 0.0).astype(BF16)

        index = lax.axis_index("mp")
        for k in range(pairs):
            at = lax.rem(index // 2 - k + levels, pairs)
            rows = pl.ds(pl.multiple_of(at * half, half), half)
            spread_rows = [spread_ref[i, rows, :] for i in range(4)]
            delta = sum(
                jnp.dot(
                    spread_rows[i],
                    panel_refs[i][...].reshape(count * quarter, tile),
                    preferred_element_type=F32,
                )
                for i in range(4)
            )
            base = keep_refs[k][...] + receive_refs[k][...].astype(F32)
            out_ref[rows, :] = (base + delta).astype(BF16)

    column = lambda i: (0, i)
    return pl.pallas_call(
        kernel,
        grid=(width // tile,),
        in_specs=[pl.BlockSpec((half, tile), column)] * (2 * pairs)
        + [VMEM, VMEM]
        + [pl.BlockSpec((count, quarter, tile), lambda i: (0, 0, i))] * 4,
        out_specs=pl.BlockSpec((total_rows, tile), column),
        out_shape=jax.ShapeDtypeStruct((total_rows, width), BF16),
        scratch_shapes=[pltpu.VMEM((4, total_rows, count * quarter), BF16)],
        compiler_params=params(12),
        name="finish",
        cost_estimate=pl.CostEstimate(
            flops=2 * total_rows * count * rank * width,
            bytes_accessed=2 * count * rank * width + 8 * total_rows * width,
            transcendentals=0,
        ),
    )(*keeps, *receives, low, store_row, *panels)


def swap(axis, size):
    def move(value):
        return lax.ppermute(value, axis, [(i, i ^ 1) for i in range(size)])

    return move


def per_device(tokens, gate, down, up, request_index, store_rows):
    count = store_rows.shape[0]
    levels = count // 2
    pairs = levels // 2
    shard = tokens.shape[0]
    own_tokens = shard * count // 2
    groups = lax.axis_size("groups")
    along_y = swap("mp", count)
    other_core = swap("sub", 2)
    other_group = swap("groups", groups)

    def along_z(value):
        return lax.ppermute(value, "mp", [(i, (i + 2) % count) for i in range(count)])

    near = [tokens]
    far = [along_y(tokens)]
    for _ in range(levels - 1):
        near.append(along_z(near[-1]))
        far.append(along_y(near[-1]))

    row_of_request = jnp.sum(
        jnp.where(
            request_index == jnp.arange(count, dtype=jnp.int32)[None, :], store_rows[None, :], 0
        ),
        axis=1,
    )
    begin = lax.axis_index("sub") * (own_tokens // 2)
    row_of_request = lax.dynamic_slice_in_dim(row_of_request, begin, own_tokens // 2, 0)
    store_row = jnp.broadcast_to(row_of_request[:, None], (own_tokens // 2, 2)).reshape(
        own_tokens, 1
    )

    quarter = lax.all_to_all(
        split_panels(up, count, groups), "mp", split_axis=0, concat_axis=0, tiled=True
    )
    quarter_x = other_group(quarter)
    panels = [quarter, quarter_x, other_core(quarter), other_core(quarter_x)]

    keeps, receives, low_keeps, low_receives = [], [], [], []
    for k in range(pairs):
        chunks = (near[k], far[k], near[k + pairs], far[k + pairs])
        low_keep, low_send = low_pair(chunks, down, k, levels)
        low_keeps.append(low_keep)
        low_receives.append(other_core(low_send))
        keep, send = base_pair(chunks, gate, k, levels)
        keeps.append(keep)
        receives.append(other_core(send))

    low = low_own(low_keeps, low_receives, store_row, levels)
    bit = 1
    while bit < count:
        low = low + lax.ppermute(low, "mp", [(i, i ^ bit) for i in range(count)])
        bit *= 2
    return finish(keeps, receives, low, store_row, panels, levels)


def solution(mesh):
    return jax.shard_map(
        per_device,
        mesh=mesh,
        in_specs=(
            P(("groups", "mp"), "sub"),
            P("sub", "mp"),
            P("mp", "sub", None),
            P("mp", None, None),
            P("groups", None),
            P(),
        ),
        out_specs=P(("groups", "sub"), "mp"),
        check_vma=False,
    )
```

```python
import jax
import jax.numpy as jnp
from jax import lax
from jax.experimental import pallas as pl
from jax.experimental.pallas import tpu as pltpu
from jax.sharding import PartitionSpec as P

F32 = jnp.float32
BF16 = jnp.bfloat16
ANY = pl.BlockSpec(memory_space=pl.ANY)
VMEM = pl.BlockSpec(memory_space=pltpu.VMEM)
ROWS_BY_ROWS = (((1,), (1,)), ((), ()))


def in_vmem(*values):
    return [pltpu.with_memory_space_constraint(value, pltpu.VMEM) for value in values]


def params(mib):
    return pltpu.CompilerParams(vmem_limit_bytes=mib << 20)


def run_copies(copies):
    for copy in copies:
        copy.start()
    for copy in copies:
        copy.wait()


def in_hbm(*values):
    return [pltpu.with_memory_space_constraint(value, pltpu.HBM) for value in values]


def position(levels):
    index = lax.axis_index("mp")
    return index // 2, lax.rem(index, 2)


def rows_of_tokens(requests, store_rows, tokens):
    count = requests.shape[1]

    def kernel(requests_ref, rows_ref, out_ref):
        request = requests_ref[...]
        row = jnp.zeros_like(request)
        for i in range(store_rows.shape[0]):
            row = jnp.where(request == i, rows_ref[i], row)
        token = lax.axis_index("sub") * tokens + lax.broadcasted_iota(
            jnp.int32, (tokens, count), 0
        )
        own = token // 2 == lax.broadcasted_iota(jnp.int32, (tokens, count), 1)
        chosen = jnp.where(own, row.astype(F32), 0.0)
        out_ref[...] = jnp.sum(chosen, axis=1, keepdims=True).astype(jnp.int32)

    return pl.pallas_call(
        kernel,
        in_specs=[VMEM, pl.BlockSpec(memory_space=pltpu.SMEM)],
        out_specs=VMEM,
        out_shape=jax.ShapeDtypeStruct((tokens, 1), jnp.int32),
        compiler_params=params(6),
        name="rows_of_tokens",
    )(requests, store_rows)


def split_panels(up, offsets, levels):
    rank, hidden = up.shape[1], up.shape[2]
    quarter, width = rank // 4, hidden // (2 * levels)

    def kernel(up_ref, *refs):
        out_refs, sem = refs[:-1], refs[-1]
        z, y = position(levels)
        which = 2 * lax.rem(lax.axis_index("groups"), 2) + lax.axis_index("sub")
        rows = pl.ds(pl.multiple_of(which * quarter, quarter), quarter)
        copies = []
        for i, (dz, dy) in enumerate(offsets):
            to = 2 * lax.rem(z + dz, levels) + (1 - y if dy else y)
            columns = pl.ds(pl.multiple_of(to * width, 128), width)
            copies.append(
                pltpu.make_async_copy(up_ref.at[0, rows, columns], out_refs[i], sem.at[i])
            )
        run_copies(copies)

    return pl.pallas_call(
        kernel,
        in_specs=[ANY],
        out_specs=[VMEM] * len(offsets),
        out_shape=[jax.ShapeDtypeStruct((quarter, width), BF16)] * len(offsets),
        scratch_shapes=[pltpu.SemaphoreType.DMA((len(offsets),))],
        compiler_params=params(6),
        name="split_panels",
    )(*in_hbm(up))


def stack(blocks):
    count = len(blocks)

    def kernel(*refs):
        run_copies(
            [pltpu.make_async_copy(refs[i], refs[count].at[i], refs[-1].at[i]) for i in range(count)]
        )

    return pl.pallas_call(
        kernel,
        in_specs=[ANY] * count,
        out_specs=VMEM,
        out_shape=jax.ShapeDtypeStruct((count, *blocks[0].shape), BF16),
        scratch_shapes=[pltpu.SemaphoreType.DMA((count,))],
        compiler_params=params(6),
        name="stack",
    )(*blocks)


HELD, PARTS = 5, 7


def hold_gate(gate):
    depth, width = gate.shape
    columns = width // PARTS * HELD
    pieces = 8

    def kernel(gate_ref, out_ref, mark_ref, sem):
        mark_ref[...] = jnp.zeros_like(mark_ref)
        size = depth // pieces
        run_copies(
            [
                pltpu.make_async_copy(
                    gate_ref.at[pl.ds(i * size, size), pl.ds(0, columns)],
                    out_ref.at[pl.ds(i * size, size)],
                    sem.at[i],
                )
                for i in range(pieces)
            ]
        )

    return pl.pallas_call(
        kernel,
        in_specs=[ANY],
        out_specs=[VMEM, VMEM],
        out_shape=[pltpu.VMEM((depth, columns), BF16), jax.ShapeDtypeStruct((8, 128), F32)],
        scratch_shapes=[pltpu.SemaphoreType.DMA((pieces,))],
        compiler_params=params(6),
        name="hold_gate",
    )(gate)


def keeps_first(step, levels):
    origin = lax.rem(position(levels)[0] - step + levels, levels)
    return (origin // (levels // 2)) == lax.axis_index("sub")


def pair_rows(step, levels, half):
    at = lax.rem(position(levels)[0] - step + levels, levels // 2)
    return pl.ds(pl.multiple_of(at * half, half), half)


def load_rows(near_ref, far_ref, rows_ref):
    shard = near_ref.shape[0]
    y = position(2)[1]
    rows_ref[pl.ds(pl.multiple_of(y * shard, shard), shard), :] = near_ref[...]
    rows_ref[pl.ds(pl.multiple_of((1 - y) * shard, shard), shard), :] = far_ref[...]


def base_chunk(near, far, gate, held, pair, down, step, levels, after=None):
    shard, depth = near.shape
    width = gate.shape[1]
    tile = width // PARTS
    piece = tile // 2
    pieces = 2 * (PARTS - HELD)
    assert pieces < HELD
    half = 2 * shard
    inputs = in_vmem(*pair, held) + [gate, near, far]
    outputs = [pltpu.VMEM((half, width), F32), pltpu.VMEM((half, width), BF16)]
    if after is not None:
        inputs.append(after)
    if down is not None:
        inputs.append(down)
        outputs.append(jax.ShapeDtypeStruct((half, down.shape[1]), F32))

    def kernel(*refs):
        held_ref, gate_ref, near_ref, far_ref = refs[len(pair) : len(pair) + 4]
        out_refs, (rows_ref, piece_ref, sem) = refs[len(inputs) : -3], refs[-3:]
        mine = keeps_first(step, levels)
        at = pl.program_id(0)

        def fetch(i):
            begin = pl.multiple_of(HELD * tile + i * piece, piece)
            slot = lax.rem(i, 2)
            return pltpu.make_async_copy(
                gate_ref.at[:, pl.ds(begin, piece)], piece_ref.at[slot], sem.at[slot]
            )

        def put(begin, size, total):
            columns = pl.ds(pl.multiple_of(begin, size), size)

            @pl.when(mine)
            def _():
                out_refs[0][:, columns] = total

            @pl.when(jnp.logical_not(mine))
            def _():
                out_refs[1][:, columns] = total.astype(BF16)

        @pl.when(at == 0)
        def _():
            fetch(0).start()
            fetch(1).start()
            load_rows(near_ref, far_ref, rows_ref)
            if down is not None:
                out_refs[-1][...] = lax.dot_general(
                    rows_ref[...],
                    refs[len(inputs) - 1][0],
                    ROWS_BY_ROWS,
                    preferred_element_type=F32,
                )

        columns = pl.ds(pl.multiple_of(at * tile, tile), tile)
        put(
            at * tile,
            tile,
            jnp.dot(rows_ref[...], held_ref[:, columns], preferred_element_type=F32),
        )

        @pl.when((at > 0) & (at <= pieces))
        def _():
            fetch(at - 1).wait()
            total = jnp.dot(
                rows_ref[...], piece_ref[lax.rem(at - 1, 2)], preferred_element_type=F32
            )
            put(HELD * tile + (at - 1) * piece, piece, total)

            @pl.when(at + 1 < pieces)
            def _():
                fetch(at + 1).start()

    return pl.pallas_call(
        kernel,
        grid=(HELD,),
        in_specs=[VMEM] * (len(pair) + 1) + [ANY] + [VMEM] * (len(inputs) - len(pair) - 2),
        out_specs=[VMEM] * len(outputs),
        out_shape=outputs,
        scratch_shapes=[
            pltpu.VMEM((half, depth), BF16),
            pltpu.VMEM((2, depth, piece), BF16),
            pltpu.SemaphoreType.DMA((2,)),
        ],
        input_output_aliases={0: 0, 1: 1} if pair else {},
        compiler_params=params(10),
        name="base_chunk",
    )(*inputs)


def low_last(near, far, down, lows, levels):
    shard, depth = near.shape
    rank = down.shape[1]
    half = 2 * shard
    pairs = levels // 2

    def kernel(*refs):
        near_ref, far_ref, down_ref = refs[:3]
        low_refs = refs[3 : 2 + levels]
        keep_ref, send_ref, rows_ref = refs[2 + levels :]
        load_rows(near_ref, far_ref, rows_ref)
        last = lax.dot_general(
            rows_ref[...], down_ref[0], ROWS_BY_ROWS, preferred_element_type=F32
        )
        for k in range(pairs):
            rows = pair_rows(k, levels, half)
            first = low_refs[k][...]
            second = last if k == pairs - 1 else low_refs[k + pairs][...]
            mine = keeps_first(k, levels)
            keep_ref[rows, :] = jnp.where(mine, first, second)
            send_ref[rows, :] = jnp.where(mine, second, first)

    return pl.pallas_call(
        kernel,
        in_specs=[VMEM] * (2 + levels),
        out_specs=[VMEM] * 2,
        out_shape=[jax.ShapeDtypeStruct((pairs * half, rank), F32)] * 2,
        scratch_shapes=[pltpu.VMEM((half, depth), BF16)],
        compiler_params=params(6),
        name="low_last",
    )(near, far, down, *lows)


def low_own(keep, receive, store_row):
    def kernel(keep_ref, receive_ref, row_ref, out_ref):
        total = keep_ref[...] + receive_ref[...]
        out_ref[...] = jnp.where(row_ref[...] == lax.axis_index("mp"), total, 0.0).astype(BF16)

    return pl.pallas_call(
        kernel,
        in_specs=[VMEM] * 3,
        out_specs=VMEM,
        out_shape=jax.ShapeDtypeStruct(keep.shape, BF16),
        compiler_params=params(6),
        name="low_own",
    )(keep, receive, store_row)


def add(one, two):
    def kernel(one_ref, two_ref, out_ref):
        out_ref[...] = one_ref[...] + two_ref[...]

    return pl.pallas_call(
        kernel,
        in_specs=[VMEM] * 2,
        out_specs=VMEM,
        out_shape=jax.ShapeDtypeStruct(one.shape, one.dtype),
        compiler_params=params(6),
        name="add",
    )(one, two)


def finish(keeps, receives, lows, store_row, panels, offsets, levels):
    half, width = keeps[0].shape
    pairs = levels // 2
    total_rows, rank = lows[0].shape
    quarter = rank // 4
    parts = len(panels[0])
    blocks = len(offsets)
    tile = 512 if width % 512 == 0 else 256
    flat = [array for group in panels for array in group]

    def kernel(*refs):
        keep_refs, receive_refs = refs[:pairs], refs[pairs : 2 * pairs]
        row_ref = refs[2 * pairs]
        panel_refs = refs[2 * pairs + 1 : 2 * pairs + 1 + len(flat)]
        low_refs = refs[2 * pairs + 1 + len(flat) : -2]
        out_ref, spread_ref = refs[-2:]

        @pl.when(pl.program_id(0) == 0)
        def _():
            low = low_refs[0][...]
            for other in low_refs[1:]:
                low = low + other[...]
            group, core = lax.rem(lax.axis_index("groups"), 2), lax.axis_index("sub")
            z, y = position(levels)
            span = blocks * quarter
            at = lax.broadcasted_iota(jnp.int32, (rank, span), 0)
            to = lax.broadcasted_iota(jnp.int32, (rank, span), 1)
            block = lax.broadcasted_iota(jnp.int32, (total_rows, span), 1) // quarter
            row = jnp.zeros((total_rows, span), jnp.int32)
            for i, (dz, dy) in enumerate(offsets):
                source = 2 * lax.rem(z - dz + levels, levels) + (1 - y if dy else y)
                row = jnp.where(block == i, source, row)
            mine = row == row_ref[...]
            for i, (own_group, own_core) in enumerate(
                ((True, True), (False, True), (True, False), (False, False))
            ):
                which = 2 * (group if own_group else 1 - group) + (core if own_core else 1 - core)
                picks = (at == which * quarter + lax.rem(to, quarter)).astype(BF16)
                spread = jnp.dot(low, picks, preferred_element_type=F32)
                spread = jnp.where(mine, spread, 0.0).astype(BF16)
                spread_ref[:, i * span : (i + 1) * span] = spread

        panel = jnp.concatenate(
            [ref[...].reshape(ref.shape[0] * quarter, tile) for ref in panel_refs], axis=0
        )
        columns = pl.ds(pl.multiple_of(pl.program_id(0) * tile, tile), tile)
        for k in range(pairs):
            rows = pair_rows(k, levels, half)
            delta = jnp.dot(spread_ref[rows, :], panel, preferred_element_type=F32)
            base = keep_refs[k][:, columns] + receive_refs[k][...].astype(F32)
            out_ref[rows, :] = (base + delta).astype(BF16)

    column = lambda i: (0, i)
    return pl.pallas_call(
        kernel,
        grid=(width // tile,),
        in_specs=[VMEM] * pairs
        + [pl.BlockSpec((half, tile), column)] * pairs
        + [VMEM]
        + [pl.BlockSpec((array.shape[0], quarter, tile), lambda i: (0, 0, i)) for array in flat]
        + [VMEM] * len(lows),
        out_specs=pl.BlockSpec((total_rows, tile), column),
        out_shape=jax.ShapeDtypeStruct((total_rows, width), BF16),
        scratch_shapes=[pltpu.VMEM((total_rows, blocks * rank), BF16)],
        compiler_params=params(10),
        name="finish",
    )(*in_vmem(*keeps), *receives, store_row, *flat, *lows)


def swap(axis, size):
    def move(value):
        return lax.ppermute(value, axis, [(i, i ^ 1) for i in range(size)])

    return move


def per_device(tokens, gate, down, up, request_index, store_rows):
    count = store_rows.shape[0]
    levels = count // 2
    pairs = levels // 2
    shard = tokens.shape[0]
    own_tokens = shard * count // 2
    along_y = swap("mp", count)
    other_core = swap("sub", 2)
    other_group = swap("groups", lax.axis_size("groups"))
    together = lax.optimization_barrier
    down = jnp.swapaxes(down, 1, 2)

    def along_mp(value, dz, dy=0):
        pairs_of = [(i, 2 * ((i // 2 + dz) % levels) + ((i % 2) ^ dy)) for i in range(count)]
        return lax.ppermute(value, "mp", pairs_of)

    store_row = rows_of_tokens(request_index.reshape(1, -1), store_rows, own_tokens)

    straight = [(dz, 0) for dz in range(levels) if dz != pairs]
    crossing = [(dz, 1) for dz in range(levels) if dz != pairs]
    middle = [(pairs, 0), (pairs, 1)]
    offsets = straight + crossing + middle
    blocks = dict(zip(offsets, split_panels(up, offsets, levels)))

    def move_blocks(chosen):
        for dz, dy in chosen:
            if (dz, dy) != (0, 0):
                blocks[dz, dy] = along_mp(blocks[dz, dy], dz, dy)

    held, mark = hold_gate(gate)
    pair_left, lows, keeps, receives, chunks = {}, [], [], [], []

    def multiply(k, near, far, down, after=None):
        made = base_chunk(near, far, gate, held, pair_left.get(k % pairs, ()), down, k, levels, after)
        pair_left[k % pairs] = made[:2]
        if down is not None:
            lows.append(made[-1])
        if k >= pairs:
            keeps.append(made[0])
            receives.append(other_core(made[1]))

    near = tokens
    for stage in range(levels):
        far = along_y(near)
        after = along_mp(near, 1) if stage < levels - 1 else near
        if stage == 0:
            move_blocks(straight + crossing[:1])
            bound = [store_row, mark]
        else:
            multiply(stage - 1, *chunks[-1], down, mark if stage == 1 else None)
            bound = [lows[-1]]
        if stage == levels - 1:
            first = stack([blocks[offset] for offset in straight + crossing])
            first_x, first_c = other_group(first), other_core(first)
            move_blocks(middle)
        elif stage > 0:
            move_blocks(crossing[stage : stage + 1])
        names = list(blocks)
        near, after, far, moved, bound = together(
            (near, after, far, [blocks[name] for name in names], bound)
        )
        blocks = dict(zip(names, moved))
        if stage == 0:
            store_row, mark = bound
        else:
            lows[-1] = bound[0]
        chunks.append((near, far))
        near = after

    near, far = chunks[-1]
    low_keep, low_send = low_last(near, far, down, lows, levels)
    low_send, second = together((low_send, stack([blocks[offset] for offset in middle])))
    second_x, second_c = other_group(second), other_core(second)
    low = low_own(low_keep, other_core(low_send), store_row)
    low, second_x, near, far = together((add(low, along_y(low)), second_x, near, far))
    parts = [low] + [along_mp(low, j) for j in range(1, levels)]
    multiply(levels - 1, near, far, None)
    panels = [
        (first, second),
        (first_x, second_x),
        (first_c, second_c),
        (other_core(first_x), other_core(second_x)),
    ]
    return finish(keeps, receives, parts, store_row, panels, offsets, levels)


def solution(mesh):
    return jax.shard_map(
        per_device,
        mesh=mesh,
        in_specs=(
            P(("groups", "mp"), "sub"),
            P("sub", "mp"),
            P("mp", "sub", None),
            P("mp", None, None),
            P("groups", None),
            P(),
        ),
        out_specs=P(("groups", "sub"), "mp"),
        check_vma=False,
    )
```

```python
import jax
import jax.numpy as jnp
from jax import lax
from jax.experimental import pallas as pl
from jax.experimental.pallas import tpu as pltpu
from jax.sharding import PartitionSpec as P

F32 = jnp.float32
BF16 = jnp.bfloat16
ANY = pl.BlockSpec(memory_space=pl.ANY)
VMEM = pl.BlockSpec(memory_space=pltpu.VMEM)
ROWS_BY_ROWS = (((1,), (1,)), ((), ()))


def in_vmem(*values):
    return [pltpu.with_memory_space_constraint(value, pltpu.VMEM) for value in values]


def params(mib):
    return pltpu.CompilerParams(vmem_limit_bytes=mib << 20)


def run_copies(copies):
    for copy in copies:
        copy.start()
    for copy in copies:
        copy.wait()


def in_hbm(*values):
    return [pltpu.with_memory_space_constraint(value, pltpu.HBM) for value in values]


def position(levels):
    index = lax.axis_index("mp")
    return index // 2, lax.rem(index, 2)


def rows_of_tokens(requests, store_rows, tokens):
    count = requests.shape[1]

    def kernel(requests_ref, rows_ref, out_ref):
        request = requests_ref[...]
        row = jnp.zeros_like(request)
        for i in range(store_rows.shape[0]):
            row = jnp.where(request == i, rows_ref[i], row)
        token = lax.axis_index("sub") * tokens + lax.broadcasted_iota(
            jnp.int32, (tokens, count), 0
        )
        own = token // 2 == lax.broadcasted_iota(jnp.int32, (tokens, count), 1)
        chosen = jnp.where(own, row.astype(F32), 0.0)
        out_ref[...] = jnp.sum(chosen, axis=1, keepdims=True).astype(jnp.int32)

    return pl.pallas_call(
        kernel,
        in_specs=[VMEM, pl.BlockSpec(memory_space=pltpu.SMEM)],
        out_specs=VMEM,
        out_shape=jax.ShapeDtypeStruct((tokens, 1), jnp.int32),
        compiler_params=params(6),
        name="rows_of_tokens",
    )(requests, store_rows)


def split_panels(up, offsets, levels):
    rank, hidden = up.shape[1], up.shape[2]
    quarter, width = rank // 4, hidden // (2 * levels)

    def kernel(up_ref, *refs):
        out_refs, sem = refs[:-1], refs[-1]
        z, y = position(levels)
        which = 2 * lax.rem(lax.axis_index("groups"), 2) + lax.axis_index("sub")
        rows = pl.ds(pl.multiple_of(which * quarter, quarter), quarter)
        copies = []
        for i, (dz, dy) in enumerate(offsets):
            to = 2 * lax.rem(z + dz, levels) + (1 - y if dy else y)
            columns = pl.ds(pl.multiple_of(to * width, 128), width)
            copies.append(
                pltpu.make_async_copy(up_ref.at[0, rows, columns], out_refs[i], sem.at[i])
            )
        run_copies(copies)

    return pl.pallas_call(
        kernel,
        in_specs=[ANY],
        out_specs=[VMEM] * len(offsets),
        out_shape=[jax.ShapeDtypeStruct((quarter, width), BF16)] * len(offsets),
        scratch_shapes=[pltpu.SemaphoreType.DMA((len(offsets),))],
        compiler_params=params(6),
        name="split_panels",
    )(*in_hbm(up))


def stack(blocks):
    count = len(blocks)

    def kernel(*refs):
        run_copies(
            [pltpu.make_async_copy(refs[i], refs[count].at[i], refs[-1].at[i]) for i in range(count)]
        )

    return pl.pallas_call(
        kernel,
        in_specs=[ANY] * count,
        out_specs=VMEM,
        out_shape=jax.ShapeDtypeStruct((count, *blocks[0].shape), BF16),
        scratch_shapes=[pltpu.SemaphoreType.DMA((count,))],
        compiler_params=params(6),
        name="stack",
    )(*blocks)


HELD, PARTS = 5, 7


def hold_gate(gate):
    depth, width = gate.shape
    columns = width // PARTS * HELD
    pieces = 8

    def kernel(gate_ref, out_ref, mark_ref, sem):
        mark_ref[...] = jnp.zeros_like(mark_ref)
        size = depth // pieces
        run_copies(
            [
                pltpu.make_async_copy(
                    gate_ref.at[pl.ds(i * size, size), pl.ds(0, columns)],
                    out_ref.at[pl.ds(i * size, size)],
                    sem.at[i],
                )
                for i in range(pieces)
            ]
        )

    return pl.pallas_call(
        kernel,
        in_specs=[ANY],
        out_specs=[VMEM, VMEM],
        out_shape=[pltpu.VMEM((depth, columns), BF16), jax.ShapeDtypeStruct((8, 128), F32)],
        scratch_shapes=[pltpu.SemaphoreType.DMA((pieces,))],
        compiler_params=params(6),
        name="hold_gate",
    )(gate)


def keeps_first(step, levels):
    origin = lax.rem(position(levels)[0] - step + levels, levels)
    return (origin // (levels // 2)) == lax.axis_index("sub")


def pair_rows(step, levels, half):
    at = lax.rem(position(levels)[0] - step + levels, levels // 2)
    return pl.ds(pl.multiple_of(at * half, half), half)


def load_rows(near_ref, far_ref, rows_ref):
    shard = near_ref.shape[0]
    y = position(2)[1]
    rows_ref[pl.ds(pl.multiple_of(y * shard, shard), shard), :] = near_ref[...]
    rows_ref[pl.ds(pl.multiple_of((1 - y) * shard, shard), shard), :] = far_ref[...]


def base_chunk(near, far, gate, held, pair, down, step, levels, after=None, tiles="all"):
    shard, depth = near.shape
    width = gate.shape[1]
    tile = width // PARTS
    piece = tile // 2
    pieces = 2 * (PARTS - HELD)
    assert pieces < HELD
    half = 2 * shard
    inputs = in_vmem(*pair, held) + [gate, near, far]
    outputs = [pltpu.VMEM((half, width), F32), pltpu.VMEM((half, width), BF16)]
    if after is not None:
        inputs.append(after)
    if down is not None:
        inputs.append(down)
        outputs.append(jax.ShapeDtypeStruct((half, down.shape[1]), F32))

    def kernel(*refs):
        held_ref, gate_ref, near_ref, far_ref = refs[len(pair) : len(pair) + 4]
        out_refs, (rows_ref, piece_ref, sem) = refs[len(inputs) : -3], refs[-3:]
        mine = keeps_first(step, levels)
        at = pl.program_id(0)

        def fetch(i):
            begin = pl.multiple_of(HELD * tile + i * piece, piece)
            slot = lax.rem(i, 2)
            return pltpu.make_async_copy(
                gate_ref.at[:, pl.ds(begin, piece)], piece_ref.at[slot], sem.at[slot]
            )

        def put(begin, size, total):
            columns = pl.ds(pl.multiple_of(begin, size), size)

            @pl.when(mine)
            def _():
                out_refs[0][:, columns] = total

            @pl.when(jnp.logical_not(mine))
            def _():
                out_refs[1][:, columns] = total.astype(BF16)

        @pl.when(at == 0)
        def _():
            if tiles != "held":
                fetch(0).start()
                fetch(1).start()
            load_rows(near_ref, far_ref, rows_ref)
            if down is not None:
                out_refs[-1][...] = lax.dot_general(
                    rows_ref[...],
                    refs[len(inputs) - 1][0],
                    ROWS_BY_ROWS,
                    preferred_element_type=F32,
                )

        if tiles != "streamed":
            columns = pl.ds(pl.multiple_of(at * tile, tile), tile)
            put(
                at * tile,
                tile,
                jnp.dot(rows_ref[...], held_ref[:, columns], preferred_element_type=F32),
            )

        if tiles != "held":
            turn = at if tiles == "streamed" else at - 1

            @pl.when((turn >= 0) & (turn < pieces))
            def _():
                fetch(turn).wait()
                total = jnp.dot(
                    rows_ref[...], piece_ref[lax.rem(turn, 2)], preferred_element_type=F32
                )
                put(HELD * tile + turn * piece, piece, total)

                @pl.when(turn + 2 < pieces)
                def _():
                    fetch(turn + 2).start()

    return pl.pallas_call(
        kernel,
        grid=(pieces if tiles == "streamed" else HELD,),
        in_specs=[VMEM] * (len(pair) + 1) + [ANY] + [VMEM] * (len(inputs) - len(pair) - 2),
        out_specs=[VMEM] * len(outputs),
        out_shape=outputs,
        scratch_shapes=[
            pltpu.VMEM((half, depth), BF16),
            pltpu.VMEM((2, depth, piece), BF16),
            pltpu.SemaphoreType.DMA((2,)),
        ],
        input_output_aliases={0: 0, 1: 1} if pair else {},
        compiler_params=params(10),
        name="base_chunk",
    )(*inputs)


def low_last(near, far, down, lows, levels):
    shard, depth = near.shape
    rank = down.shape[1]
    half = 2 * shard
    pairs = levels // 2

    def kernel(*refs):
        near_ref, far_ref, down_ref = refs[:3]
        low_refs = refs[3 : 2 + levels]
        keep_ref, send_ref, rows_ref = refs[2 + levels :]
        load_rows(near_ref, far_ref, rows_ref)
        last = lax.dot_general(
            rows_ref[...], down_ref[0], ROWS_BY_ROWS, preferred_element_type=F32
        )
        for k in range(pairs):
            rows = pair_rows(k, levels, half)
            first = low_refs[k][...]
            second = last if k == pairs - 1 else low_refs[k + pairs][...]
            mine = keeps_first(k, levels)
            keep_ref[rows, :] = jnp.where(mine, first, second)
            send_ref[rows, :] = jnp.where(mine, second, first)

    return pl.pallas_call(
        kernel,
        in_specs=[VMEM] * (2 + levels),
        out_specs=[VMEM] * 2,
        out_shape=[jax.ShapeDtypeStruct((pairs * half, rank), F32)] * 2,
        scratch_shapes=[pltpu.VMEM((half, depth), BF16)],
        compiler_params=params(6),
        name="low_last",
    )(near, far, down, *lows)


def low_own(keep, receive, store_row):
    def kernel(keep_ref, receive_ref, row_ref, out_ref):
        total = keep_ref[...] + receive_ref[...]
        out_ref[...] = jnp.where(row_ref[...] == lax.axis_index("mp"), total, 0.0).astype(BF16)

    return pl.pallas_call(
        kernel,
        in_specs=[VMEM] * 3,
        out_specs=VMEM,
        out_shape=jax.ShapeDtypeStruct(keep.shape, BF16),
        compiler_params=params(6),
        name="low_own",
    )(keep, receive, store_row)


def add(one, two):
    def kernel(one_ref, two_ref, out_ref):
        out_ref[...] = one_ref[...] + two_ref[...]

    return pl.pallas_call(
        kernel,
        in_specs=[VMEM] * 2,
        out_specs=VMEM,
        out_shape=jax.ShapeDtypeStruct(one.shape, one.dtype),
        compiler_params=params(6),
        name="add",
    )(one, two)


def finish(keeps, receives, lows, store_row, panels, offsets, levels):
    half, width = keeps[0].shape
    pairs = levels // 2
    total_rows, rank = lows[0].shape
    quarter = rank // 4
    parts = len(panels[0])
    blocks = len(offsets)
    tile = width // 2
    flat = [array for group in panels for array in group]

    def kernel(*refs):
        keep_refs, receive_refs = refs[:pairs], refs[pairs : 2 * pairs]
        row_ref = refs[2 * pairs]
        panel_refs = refs[2 * pairs + 1 : 2 * pairs + 1 + len(flat)]
        low_refs = refs[2 * pairs + 1 + len(flat) : -2]
        out_ref, spread_ref = refs[-2:]

        @pl.when(pl.program_id(0) == 0)
        def _():
            low = low_refs[0][...]
            for other in low_refs[1:]:
                low = low + other[...]
            group, core = lax.rem(lax.axis_index("groups"), 2), lax.axis_index("sub")
            z, y = position(levels)
            span = blocks * quarter
            at = lax.broadcasted_iota(jnp.int32, (rank, span), 0)
            to = lax.broadcasted_iota(jnp.int32, (rank, span), 1)
            block = lax.broadcasted_iota(jnp.int32, (total_rows, span), 1) // quarter
            row = jnp.zeros((total_rows, span), jnp.int32)
            for i, (dz, dy) in enumerate(offsets):
                source = 2 * lax.rem(z - dz + levels, levels) + (1 - y if dy else y)
                row = jnp.where(block == i, source, row)
            mine = row == row_ref[...]
            for i, (own_group, own_core) in enumerate(
                ((True, True), (False, True), (True, False), (False, False))
            ):
                which = 2 * (group if own_group else 1 - group) + (core if own_core else 1 - core)
                picks = (at == which * quarter + lax.rem(to, quarter)).astype(BF16)
                spread = jnp.dot(low, picks, preferred_element_type=F32)
                spread = jnp.where(mine, spread, 0.0).astype(BF16)
                spread_ref[:, i * span : (i + 1) * span] = spread

        panel = jnp.concatenate(
            [ref[...].reshape(ref.shape[0] * quarter, tile) for ref in panel_refs], axis=0
        )
        columns = pl.ds(pl.multiple_of(pl.program_id(0) * tile, tile), tile)
        for k in range(pairs):
            rows = pair_rows(k, levels, half)
            delta = jnp.dot(spread_ref[rows, :], panel, preferred_element_type=F32)
            base = keep_refs[k][:, columns] + receive_refs[k][...].astype(F32)
            out_ref[rows, :] = (base + delta).astype(BF16)

    column = lambda i: (0, i)
    return pl.pallas_call(
        kernel,
        grid=(width // tile,),
        in_specs=[VMEM] * pairs
        + [pl.BlockSpec((half, tile), column)] * pairs
        + [VMEM]
        + [pl.BlockSpec((array.shape[0], quarter, tile), lambda i: (0, 0, i)) for array in flat]
        + [VMEM] * len(lows),
        out_specs=pl.BlockSpec((total_rows, tile), column),
        out_shape=jax.ShapeDtypeStruct((total_rows, width), BF16),
        scratch_shapes=[pltpu.VMEM((total_rows, blocks * rank), BF16)],
        compiler_params=params(16),
        name="finish",
    )(*in_vmem(*keeps), *receives, store_row, *flat, *lows)


def swap(axis, size):
    def move(value):
        return lax.ppermute(value, axis, [(i, i ^ 1) for i in range(size)])

    return move


def per_device(tokens, gate, down, up, request_index, store_rows):
    count = store_rows.shape[0]
    levels = count // 2
    pairs = levels // 2
    shard = tokens.shape[0]
    own_tokens = shard * count // 2
    along_y = swap("mp", count)
    other_core = swap("sub", 2)
    other_group = swap("groups", lax.axis_size("groups"))
    together = lax.optimization_barrier
    down = jnp.swapaxes(down, 1, 2)

    def along_mp(value, dz, dy=0):
        pairs_of = [(i, 2 * ((i // 2 + dz) % levels) + ((i % 2) ^ dy)) for i in range(count)]
        return lax.ppermute(value, "mp", pairs_of)

    store_row = rows_of_tokens(request_index.reshape(1, -1), store_rows, own_tokens)

    early = [(1, 0), (0, 1)]
    crossing = [(dz, 1) for dz in range(1, levels) if dz != pairs]
    beside_last = [(dz, 0) for dz in range(2, levels)]
    late = [(pairs, 1)]
    first_offsets = [(0, 0)] + early + crossing
    second_offsets = beside_last + late
    offsets = first_offsets + second_offsets
    blocks = dict(zip(offsets, split_panels(up, offsets, levels)))

    def move_blocks(chosen):
        for dz, dy in chosen:
            if (dz, dy) != (0, 0):
                blocks[dz, dy] = along_mp(blocks[dz, dy], dz, dy)

    held, mark = hold_gate(gate)
    pair_left, lows, chunks = {}, [], []

    def multiply(k, near, far, down, after=None, tiles="all"):
        pair = pair_left.get(k % pairs, ())
        made = base_chunk(near, far, gate, held, pair, down, k, levels, after, tiles)
        pair_left[k % pairs] = made[:2]
        if down is not None:
            lows.append(made[-1])

    near = tokens
    for stage in range(levels):
        far = along_y(near)
        after = along_mp(near, 1) if stage < levels - 1 else near
        if stage == 0:
            move_blocks(early)
            bound = [store_row, mark]
        else:
            multiply(stage - 1, *chunks[-1], down, mark if stage == 1 else None)
            bound = [lows[-1]]
        if stage == levels - 1:
            first_x, first_c = other_group(first), other_core(first)
            move_blocks(beside_last)
        elif stage > 0:
            move_blocks(crossing[stage - 1 : stage])
        names = list(blocks)
        near, after, far, moved, bound = together(
            (near, after, far, [blocks[name] for name in names], bound)
        )
        blocks = dict(zip(names, moved))
        if stage == 0:
            store_row, mark = bound
        else:
            lows[-1] = bound[0]
        if stage == levels - 2:
            first = stack([blocks[offset] for offset in first_offsets])
        chunks.append((near, far))
        near = after

    near, far = chunks[-1]
    last = levels - 1
    move_blocks(late)
    low_keep, low_send = low_last(near, far, down, lows, levels)
    low = low_own(low_keep, other_core(low_send), store_row)

    crossed = along_y(low)
    multiply(last, near, far, None, tiles="held")
    moved = [blocks[offset] for offset in second_offsets]
    low, crossed, pair_left[last % pairs], moved, first, first_x, first_c = together(
        (low, crossed, pair_left[last % pairs], moved, first, first_x, first_c)
    )
    first_xc = other_core(first_x)
    second = stack(moved)
    second_x, second_c = other_group(second), other_core(second)
    low = add(low, crossed)
    bit = 1
    while bit < levels:
        crossed = lax.ppermute(low, "mp", [(i, i ^ (2 * bit)) for i in range(count)])
        if bit == 1:
            multiply(last, near, far, None, tiles="streamed")
            low, crossed, pair_left[last % pairs], second_x = together(
                (low, crossed, pair_left[last % pairs], second_x)
            )
            receives = [other_core(pair_left[k][1]) for k in range(pairs)]
        low = add(low, crossed)
        bit *= 2
    keeps = [pair_left[k][0] for k in range(pairs)]
    parts = [low]
    panels = [
        (first, second),
        (first_x, second_x),
        (first_c, second_c),
        (first_xc, other_core(second_x)),
    ]
    return finish(keeps, receives, parts, store_row, panels, offsets, levels)


def solution(mesh):
    return jax.shard_map(
        per_device,
        mesh=mesh,
        in_specs=(
            P(("groups", "mp"), "sub"),
            P("sub", "mp"),
            P("mp", "sub", None),
            P("mp", None, None),
            P("groups", None),
            P(),
        ),
        out_specs=P(("groups", "sub"), "mp"),
        check_vma=False,
    )
```

```python
import jax
import jax.numpy as jnp
from jax import lax
from jax.experimental import pallas as pl
from jax.experimental.pallas import tpu as pltpu
from jax.sharding import PartitionSpec as P

F32 = jnp.float32
BF16 = jnp.bfloat16
ANY = pl.BlockSpec(memory_space=pl.ANY)
VMEM = pl.BlockSpec(memory_space=pltpu.VMEM)
ROWS_BY_ROWS = (((1,), (1,)), ((), ()))


def in_vmem(*values):
    return [pltpu.with_memory_space_constraint(value, pltpu.VMEM) for value in values]


def params(mib):
    return pltpu.CompilerParams(vmem_limit_bytes=mib << 20)


def run_copies(copies):
    for copy in copies:
        copy.start()
    for copy in copies:
        copy.wait()


def in_hbm(*values):
    return [pltpu.with_memory_space_constraint(value, pltpu.HBM) for value in values]


def position(levels):
    index = lax.axis_index("mp")
    return index // 2, lax.rem(index, 2)


def rows_of_tokens(requests, store_rows, tokens):
    count = requests.shape[1]

    def kernel(requests_ref, rows_ref, out_ref):
        request = requests_ref[...]
        row = jnp.zeros_like(request)
        for i in range(store_rows.shape[0]):
            row = jnp.where(request == i, rows_ref[i], row)
        token = lax.axis_index("sub") * tokens + lax.broadcasted_iota(
            jnp.int32, (tokens, count), 0
        )
        own = token // 2 == lax.broadcasted_iota(jnp.int32, (tokens, count), 1)
        chosen = jnp.where(own, row.astype(F32), 0.0)
        out_ref[...] = jnp.sum(chosen, axis=1, keepdims=True).astype(jnp.int32)

    return pl.pallas_call(
        kernel,
        in_specs=[VMEM, pl.BlockSpec(memory_space=pltpu.SMEM)],
        out_specs=VMEM,
        out_shape=jax.ShapeDtypeStruct((tokens, 1), jnp.int32),
        compiler_params=params(6),
        name="rows_of_tokens",
    )(requests, store_rows)


def split_panels(up, offsets, levels):
    rank, hidden = up.shape[1], up.shape[2]
    quarter, width = rank // 4, hidden // (2 * levels)

    def kernel(up_ref, *refs):
        out_refs, sem = refs[:-1], refs[-1]
        z, y = position(levels)
        which = 2 * lax.rem(lax.axis_index("groups"), 2) + lax.axis_index("sub")
        rows = pl.ds(pl.multiple_of(which * quarter, quarter), quarter)
        copies = []
        for i, (dz, dy) in enumerate(offsets):
            to = 2 * lax.rem(z + dz, levels) + (1 - y if dy else y)
            columns = pl.ds(pl.multiple_of(to * width, 128), width)
            copies.append(
                pltpu.make_async_copy(up_ref.at[0, rows, columns], out_refs[i], sem.at[i])
            )
        run_copies(copies)

    return pl.pallas_call(
        kernel,
        in_specs=[ANY],
        out_specs=[VMEM] * len(offsets),
        out_shape=[jax.ShapeDtypeStruct((quarter, width), BF16)] * len(offsets),
        scratch_shapes=[pltpu.SemaphoreType.DMA((len(offsets),))],
        compiler_params=params(6),
        name="split_panels",
    )(*in_hbm(up))


def stack(blocks):
    count = len(blocks)

    def kernel(*refs):
        run_copies(
            [pltpu.make_async_copy(refs[i], refs[count].at[i], refs[-1].at[i]) for i in range(count)]
        )

    return pl.pallas_call(
        kernel,
        in_specs=[ANY] * count,
        out_specs=VMEM,
        out_shape=jax.ShapeDtypeStruct((count, *blocks[0].shape), BF16),
        scratch_shapes=[pltpu.SemaphoreType.DMA((count,))],
        compiler_params=params(6),
        name="stack",
    )(*blocks)


HELD, PARTS = 5, 7


def hold_gate(gate):
    depth, width = gate.shape
    columns = width // PARTS * HELD
    pieces = 8

    def kernel(gate_ref, out_ref, mark_ref, sem):
        mark_ref[...] = jnp.zeros_like(mark_ref)
        size = depth // pieces
        run_copies(
            [
                pltpu.make_async_copy(
                    gate_ref.at[pl.ds(i * size, size), pl.ds(0, columns)],
                    out_ref.at[pl.ds(i * size, size)],
                    sem.at[i],
                )
                for i in range(pieces)
            ]
        )

    return pl.pallas_call(
        kernel,
        in_specs=[ANY],
        out_specs=[VMEM, VMEM],
        out_shape=[pltpu.VMEM((depth, columns), BF16), jax.ShapeDtypeStruct((8, 128), F32)],
        scratch_shapes=[pltpu.SemaphoreType.DMA((pieces,))],
        compiler_params=params(6),
        name="hold_gate",
    )(gate)


def keeps_first(step, levels):
    origin = lax.rem(position(levels)[0] - step + levels, levels)
    return (origin // (levels // 2)) == lax.axis_index("sub")


def pair_rows(step, levels, half):
    at = lax.rem(position(levels)[0] - step + levels, levels // 2)
    return pl.ds(pl.multiple_of(at * half, half), half)


def load_rows(near_ref, far_ref, rows_ref):
    shard = near_ref.shape[0]
    y = position(2)[1]
    rows_ref[pl.ds(pl.multiple_of(y * shard, shard), shard), :] = near_ref[...]
    rows_ref[pl.ds(pl.multiple_of((1 - y) * shard, shard), shard), :] = far_ref[...]


def base_chunk(near, far, gate, held, pair, down, step, levels, after=None, tiles="all"):
    shard, depth = near.shape
    width = gate.shape[1]
    tile = width // PARTS
    piece = tile // 2
    pieces = 2 * (PARTS - HELD)
    assert pieces < HELD
    half = 2 * shard
    inputs = in_vmem(*pair, held) + [gate, near, far]
    outputs = [pltpu.VMEM((half, width), F32), pltpu.VMEM((half, width), BF16)]
    if after is not None:
        inputs.append(after)
    if down is not None:
        inputs.append(down)
        outputs.append(jax.ShapeDtypeStruct((half, down.shape[1]), F32))

    def kernel(*refs):
        held_ref, gate_ref, near_ref, far_ref = refs[len(pair) : len(pair) + 4]
        out_refs, (rows_ref, piece_ref, sem) = refs[len(inputs) : -3], refs[-3:]
        mine = keeps_first(step, levels)
        at = pl.program_id(0)

        def fetch(i):
            begin = pl.multiple_of(HELD * tile + i * piece, piece)
            slot = lax.rem(i, 2)
            return pltpu.make_async_copy(
                gate_ref.at[:, pl.ds(begin, piece)], piece_ref.at[slot], sem.at[slot]
            )

        def put(begin, size, total):
            columns = pl.ds(pl.multiple_of(begin, size), size)

            @pl.when(mine)
            def _():
                out_refs[0][:, columns] = total

            @pl.when(jnp.logical_not(mine))
            def _():
                out_refs[1][:, columns] = total.astype(BF16)

        @pl.when(at == 0)
        def _():
            if tiles != "held":
                fetch(0).start()
                fetch(1).start()
            load_rows(near_ref, far_ref, rows_ref)
            if down is not None:
                out_refs[-1][...] = lax.dot_general(
                    rows_ref[...],
                    refs[len(inputs) - 1][0],
                    ROWS_BY_ROWS,
                    preferred_element_type=F32,
                )

        if tiles != "streamed":
            columns = pl.ds(pl.multiple_of(at * tile, tile), tile)
            put(
                at * tile,
                tile,
                jnp.dot(rows_ref[...], held_ref[:, columns], preferred_element_type=F32),
            )

        if tiles != "held":
            turn = at if tiles == "streamed" else at - 1

            @pl.when((turn >= 0) & (turn < pieces))
            def _():
                fetch(turn).wait()
                total = jnp.dot(
                    rows_ref[...], piece_ref[lax.rem(turn, 2)], preferred_element_type=F32
                )
                put(HELD * tile + turn * piece, piece, total)

                @pl.when(turn + 2 < pieces)
                def _():
                    fetch(turn + 2).start()

    return pl.pallas_call(
        kernel,
        grid=(pieces if tiles == "streamed" else HELD,),
        in_specs=[VMEM] * (len(pair) + 1) + [ANY] + [VMEM] * (len(inputs) - len(pair) - 2),
        out_specs=[VMEM] * len(outputs),
        out_shape=outputs,
        scratch_shapes=[
            pltpu.VMEM((half, depth), BF16),
            pltpu.VMEM((2, depth, piece), BF16),
            pltpu.SemaphoreType.DMA((2,)),
        ],
        input_output_aliases={0: 0, 1: 1} if pair else {},
        compiler_params=params(10),
        name="base_chunk",
    )(*inputs)


def low_last(near, far, down, lows, levels):
    shard, depth = near.shape
    rank = down.shape[1]
    half = 2 * shard
    pairs = levels // 2

    def kernel(*refs):
        near_ref, far_ref, down_ref = refs[:3]
        low_refs = refs[3 : 2 + levels]
        keep_ref, send_ref, rows_ref = refs[2 + levels :]
        load_rows(near_ref, far_ref, rows_ref)
        last = lax.dot_general(
            rows_ref[...], down_ref[0], ROWS_BY_ROWS, preferred_element_type=F32
        )
        for k in range(pairs):
            rows = pair_rows(k, levels, half)
            first = low_refs[k][...]
            second = last if k == pairs - 1 else low_refs[k + pairs][...]
            mine = keeps_first(k, levels)
            keep_ref[rows, :] = jnp.where(mine, first, second)
            send_ref[rows, :] = jnp.where(mine, second, first)

    return pl.pallas_call(
        kernel,
        in_specs=[VMEM] * (2 + levels),
        out_specs=[VMEM] * 2,
        out_shape=[jax.ShapeDtypeStruct((pairs * half, rank), F32)] * 2,
        scratch_shapes=[pltpu.VMEM((half, depth), BF16)],
        compiler_params=params(6),
        name="low_last",
    )(near, far, down, *lows)


def low_own(keep, receive, store_row):
    def kernel(keep_ref, receive_ref, row_ref, out_ref):
        total = keep_ref[...] + receive_ref[...]
        out_ref[...] = jnp.where(row_ref[...] == lax.axis_index("mp"), total, 0.0).astype(BF16)

    return pl.pallas_call(
        kernel,
        in_specs=[VMEM] * 3,
        out_specs=VMEM,
        out_shape=jax.ShapeDtypeStruct(keep.shape, BF16),
        compiler_params=params(6),
        name="low_own",
    )(keep, receive, store_row)


def add(one, two):
    def kernel(one_ref, two_ref, out_ref):
        out_ref[...] = one_ref[...] + two_ref[...]

    return pl.pallas_call(
        kernel,
        in_specs=[VMEM] * 2,
        out_specs=VMEM,
        out_shape=jax.ShapeDtypeStruct(one.shape, one.dtype),
        compiler_params=params(6),
        name="add",
    )(one, two)


def finish(keeps, receives, lows, store_row, panels, offsets, levels):
    half, width = keeps[0].shape
    pairs = levels // 2
    total_rows, rank = lows[0].shape
    quarter = rank // 4
    parts = len(panels[0])
    blocks = len(offsets)
    tile = width // 2
    flat = [array for group in panels for array in group]

    def kernel(*refs):
        keep_refs, receive_refs = refs[:pairs], refs[pairs : 2 * pairs]
        row_ref = refs[2 * pairs]
        panel_refs = refs[2 * pairs + 1 : 2 * pairs + 1 + len(flat)]
        low_refs = refs[2 * pairs + 1 + len(flat) : -2]
        out_ref, spread_ref = refs[-2:]

        @pl.when(pl.program_id(0) == 0)
        def _():
            low = low_refs[0][...]
            for other in low_refs[1:]:
                low = low + other[...]
            group, core = lax.rem(lax.axis_index("groups"), 2), lax.axis_index("sub")
            z, y = position(levels)
            span = blocks * quarter
            at = lax.broadcasted_iota(jnp.int32, (rank, span), 0)
            to = lax.broadcasted_iota(jnp.int32, (rank, span), 1)
            block = lax.broadcasted_iota(jnp.int32, (total_rows, span), 1) // quarter
            row = jnp.zeros((total_rows, span), jnp.int32)
            for i, (dz, dy) in enumerate(offsets):
                source = 2 * lax.rem(z - dz + levels, levels) + (1 - y if dy else y)
                row = jnp.where(block == i, source, row)
            mine = row == row_ref[...]
            for i, (own_group, own_core) in enumerate(
                ((True, True), (False, True), (True, False), (False, False))
            ):
                which = 2 * (group if own_group else 1 - group) + (core if own_core else 1 - core)
                picks = (at == which * quarter + lax.rem(to, quarter)).astype(BF16)
                spread = jnp.dot(low, picks, preferred_element_type=F32)
                spread = jnp.where(mine, spread, 0.0).astype(BF16)
                spread_ref[:, i * span : (i + 1) * span] = spread

        panel = jnp.concatenate(
            [ref[...].reshape(ref.shape[0] * quarter, tile) for ref in panel_refs], axis=0
        )
        columns = pl.ds(pl.multiple_of(pl.program_id(0) * tile, tile), tile)
        for k in range(pairs):
            rows = pair_rows(k, levels, half)
            delta = jnp.dot(spread_ref[rows, :], panel, preferred_element_type=F32)
            base = keep_refs[k][:, columns] + receive_refs[k][...].astype(F32)
            out_ref[rows, :] = (base + delta).astype(BF16)

    column = lambda i: (0, i)
    return pl.pallas_call(
        kernel,
        grid=(width // tile,),
        in_specs=[VMEM] * pairs
        + [pl.BlockSpec((half, tile), column)] * pairs
        + [VMEM]
        + [pl.BlockSpec((array.shape[0], quarter, tile), lambda i: (0, 0, i)) for array in flat]
        + [VMEM] * len(lows),
        out_specs=pl.BlockSpec((total_rows, tile), column),
        out_shape=jax.ShapeDtypeStruct((total_rows, width), BF16),
        scratch_shapes=[pltpu.VMEM((total_rows, blocks * rank), BF16)],
        compiler_params=params(16),
        name="finish",
    )(*in_vmem(*keeps), *receives, store_row, *flat, *lows)


def swap(axis, size):
    def move(value):
        return lax.ppermute(value, axis, [(i, i ^ 1) for i in range(size)])

    return move


def per_device(tokens, gate, down, up, request_index, store_rows):
    count = store_rows.shape[0]
    levels = count // 2
    pairs = levels // 2
    shard = tokens.shape[0]
    own_tokens = shard * count // 2
    along_y = swap("mp", count)
    other_core = swap("sub", 2)
    other_group = swap("groups", lax.axis_size("groups"))
    together = lax.optimization_barrier
    down = jnp.swapaxes(down, 1, 2)

    def along_mp(value, dz, dy=0):
        pairs_of = [(i, 2 * ((i // 2 + dz) % levels) + ((i % 2) ^ dy)) for i in range(count)]
        return lax.ppermute(value, "mp", pairs_of)

    store_row = rows_of_tokens(request_index.reshape(1, -1), store_rows, own_tokens)

    early = [(1, 0), (0, 1)]
    crossing = [(dz, 1) for dz in range(1, levels) if dz != pairs]
    beside_last = [(dz, 0) for dz in range(2, levels)]
    late = [(pairs, 1)]
    first_offsets = [(0, 0)] + early + crossing
    second_offsets = beside_last + late
    offsets = first_offsets + second_offsets
    blocks = dict(zip(offsets, split_panels(up, offsets, levels)))

    def move_blocks(chosen):
        for dz, dy in chosen:
            if (dz, dy) != (0, 0):
                blocks[dz, dy] = along_mp(blocks[dz, dy], dz, dy)

    held, mark = hold_gate(gate)
    pair_left, lows, chunks = {}, [], []

    def multiply(k, near, far, down, after=None, tiles="all"):
        pair = pair_left.get(k % pairs, ())
        made = base_chunk(near, far, gate, held, pair, down, k, levels, after, tiles)
        pair_left[k % pairs] = made[:2]
        if down is not None:
            lows.append(made[-1])

    near = tokens
    for stage in range(levels):
        far = along_y(near)
        after = along_mp(near, 1) if stage < levels - 1 else near
        if stage == 0:
            move_blocks(early)
            bound = [store_row, mark]
        else:
            multiply(stage - 1, *chunks[-1], down, mark if stage == 1 else None)
            bound = [lows[-1]]
        if stage == levels - 1:
            first_x, first_c = other_group(first), other_core(first)
            move_blocks(beside_last)
        elif stage > 0:
            move_blocks(crossing[stage - 1 : stage])
        names = list(blocks)
        near, after, far, moved, bound = together(
            (near, after, far, [blocks[name] for name in names], bound)
        )
        blocks = dict(zip(names, moved))
        if stage == 0:
            store_row, mark = bound
        else:
            lows[-1] = bound[0]
        if stage == levels - 2:
            first = stack([blocks[offset] for offset in first_offsets])
        chunks.append((near, far))
        near = after

    near, far = chunks[-1]
    last = levels - 1
    move_blocks(late)
    low_keep, low_send = low_last(near, far, down, lows, levels)
    low = low_own(low_keep, other_core(low_send), store_row)

    crossed = along_y(low)
    multiply(last, near, far, None, tiles="held")
    moved = [blocks[offset] for offset in second_offsets]
    low, crossed, pair_left[last % pairs], moved, first, first_x, first_c = together(
        (low, crossed, pair_left[last % pairs], moved, first, first_x, first_c)
    )
    first_xc = other_core(first_x)
    second = stack(moved)
    second_x, second_c = other_group(second), other_core(second)
    low = add(low, crossed)
    parts = [along_mp(low, j) for j in range(1, levels)]
    multiply(last, near, far, None, tiles="streamed")
    low, parts, pair_left[last % pairs], second_x, second_c = together(
        (low, parts, pair_left[last % pairs], second_x, second_c)
    )
    parts = [low] + parts
    receives = [other_core(pair_left[k][1]) for k in range(pairs)]
    keeps = [pair_left[k][0] for k in range(pairs)]
    panels = [
        (first, second),
        (first_x, second_x),
        (first_c, second_c),
        (first_xc, other_core(second_x)),
    ]
    return finish(keeps, receives, parts, store_row, panels, offsets, levels)


def solution(mesh):
    return jax.shard_map(
        per_device,
        mesh=mesh,
        in_specs=(
            P(("groups", "mp"), "sub"),
            P("sub", "mp"),
            P("mp", "sub", None),
            P("mp", None, None),
            P("groups", None),
            P(),
        ),
        out_specs=P(("groups", "sub"), "mp"),
        check_vma=False,
    )
```

```python
import jax
import jax.numpy as jnp
from jax import lax
from jax.experimental import pallas as pl
from jax.experimental.pallas import tpu as pltpu
from jax.sharding import PartitionSpec as P

F32 = jnp.float32
BF16 = jnp.bfloat16
ANY = pl.BlockSpec(memory_space=pl.ANY)
VMEM = pl.BlockSpec(memory_space=pltpu.VMEM)
ROWS_BY_ROWS = (((1,), (1,)), ((), ()))


def in_vmem(*values):
    return [pltpu.with_memory_space_constraint(value, pltpu.VMEM) for value in values]


def params(mib):
    return pltpu.CompilerParams(vmem_limit_bytes=mib << 20)


def run_copies(copies):
    for copy in copies:
        copy.start()
    for copy in copies:
        copy.wait()


def in_hbm(*values):
    return [pltpu.with_memory_space_constraint(value, pltpu.HBM) for value in values]


def position(levels):
    index = lax.axis_index("mp")
    return index // 2, lax.rem(index, 2)


def rows_of_tokens(requests, store_rows, tokens):
    count = requests.shape[1]

    def kernel(requests_ref, rows_ref, out_ref):
        request = requests_ref[...]
        row = jnp.zeros_like(request)
        for i in range(store_rows.shape[0]):
            row = jnp.where(request == i, rows_ref[i], row)
        token = lax.axis_index("sub") * tokens + lax.broadcasted_iota(
            jnp.int32, (tokens, count), 0
        )
        own = token // 2 == lax.broadcasted_iota(jnp.int32, (tokens, count), 1)
        chosen = jnp.where(own, row.astype(F32), 0.0)
        out_ref[...] = jnp.sum(chosen, axis=1, keepdims=True).astype(jnp.int32)

    return pl.pallas_call(
        kernel,
        in_specs=[VMEM, pl.BlockSpec(memory_space=pltpu.SMEM)],
        out_specs=VMEM,
        out_shape=jax.ShapeDtypeStruct((tokens, 1), jnp.int32),
        compiler_params=params(6),
        name="rows_of_tokens",
    )(requests, store_rows)


def split_panels(up, offsets, levels):
    rank, hidden = up.shape[1], up.shape[2]
    quarter, width = rank // 4, hidden // (2 * levels)

    def kernel(up_ref, *refs):
        out_refs, sem = refs[:-1], refs[-1]
        z, y = position(levels)
        which = 2 * lax.rem(lax.axis_index("groups"), 2) + lax.axis_index("sub")
        rows = pl.ds(pl.multiple_of(which * quarter, quarter), quarter)
        copies = []
        for i, (dz, dy) in enumerate(offsets):
            to = 2 * lax.rem(z + dz, levels) + (1 - y if dy else y)
            columns = pl.ds(pl.multiple_of(to * width, 128), width)
            copies.append(
                pltpu.make_async_copy(up_ref.at[0, rows, columns], out_refs[i], sem.at[i])
            )
        run_copies(copies)

    return pl.pallas_call(
        kernel,
        in_specs=[ANY],
        out_specs=[VMEM] * len(offsets),
        out_shape=[jax.ShapeDtypeStruct((quarter, width), BF16)] * len(offsets),
        scratch_shapes=[pltpu.SemaphoreType.DMA((len(offsets),))],
        compiler_params=params(6),
        name="split_panels",
    )(*in_hbm(up))


def stack(blocks):
    count = len(blocks)

    def kernel(*refs):
        run_copies(
            [pltpu.make_async_copy(refs[i], refs[count].at[i], refs[-1].at[i]) for i in range(count)]
        )

    return pl.pallas_call(
        kernel,
        in_specs=[ANY] * count,
        out_specs=VMEM,
        out_shape=jax.ShapeDtypeStruct((count, *blocks[0].shape), BF16),
        scratch_shapes=[pltpu.SemaphoreType.DMA((count,))],
        compiler_params=params(6),
        name="stack",
    )(*blocks)


HELD, PARTS = 5, 7


def hold_gate(gate):
    depth, width = gate.shape
    columns = width // PARTS * HELD
    pieces = 8

    def kernel(gate_ref, out_ref, mark_ref, sem):
        mark_ref[...] = jnp.zeros_like(mark_ref)
        size = depth // pieces
        run_copies(
            [
                pltpu.make_async_copy(
                    gate_ref.at[pl.ds(i * size, size), pl.ds(0, columns)],
                    out_ref.at[pl.ds(i * size, size)],
                    sem.at[i],
                )
                for i in range(pieces)
            ]
        )

    return pl.pallas_call(
        kernel,
        in_specs=[ANY],
        out_specs=[VMEM, VMEM],
        out_shape=[pltpu.VMEM((depth, columns), BF16), jax.ShapeDtypeStruct((8, 128), F32)],
        scratch_shapes=[pltpu.SemaphoreType.DMA((pieces,))],
        compiler_params=params(6),
        name="hold_gate",
    )(gate)


def keeps_first(step, levels):
    origin = lax.rem(position(levels)[0] - step + levels, levels)
    return (origin // (levels // 2)) == lax.axis_index("sub")


def pair_rows(step, levels, half):
    at = lax.rem(position(levels)[0] - step + levels, levels // 2)
    return pl.ds(pl.multiple_of(at * half, half), half)


def load_rows(near_ref, far_ref, rows_ref):
    shard = near_ref.shape[0]
    y = position(2)[1]
    rows_ref[pl.ds(pl.multiple_of(y * shard, shard), shard), :] = near_ref[...]
    rows_ref[pl.ds(pl.multiple_of((1 - y) * shard, shard), shard), :] = far_ref[...]


def base_chunk(near, far, gate, held, pair, down, step, levels, after=None, tiles="all"):
    shard, depth = near.shape
    width = gate.shape[1]
    tile = width // PARTS
    piece = tile // 2
    pieces = 2 * (PARTS - HELD)
    assert pieces < HELD
    slots = pieces if tiles == "streamed" else 2
    half = 2 * shard
    inputs = in_vmem(*pair, held) + [gate, near, far]
    outputs = [pltpu.VMEM((half, width), F32), pltpu.VMEM((half, width), BF16)]
    if after is not None:
        inputs.append(after)
    if down is not None:
        inputs.append(down)
        outputs.append(jax.ShapeDtypeStruct((half, down.shape[1]), F32))

    def kernel(*refs):
        held_ref, gate_ref, near_ref, far_ref = refs[len(pair) : len(pair) + 4]
        out_refs, (rows_ref, piece_ref, sem) = refs[len(inputs) : -3], refs[-3:]
        mine = keeps_first(step, levels)
        at = pl.program_id(0)

        def fetch(i):
            begin = pl.multiple_of(HELD * tile + i * piece, piece)
            slot = lax.rem(i, slots)
            return pltpu.make_async_copy(
                gate_ref.at[:, pl.ds(begin, piece)], piece_ref.at[slot], sem.at[slot]
            )

        def put(begin, size, total):
            columns = pl.ds(pl.multiple_of(begin, size), size)

            @pl.when(mine)
            def _():
                out_refs[0][:, columns] = total

            @pl.when(jnp.logical_not(mine))
            def _():
                out_refs[1][:, columns] = total.astype(BF16)

        @pl.when(at == 0)
        def _():
            if tiles != "held":
                for i in range(slots):
                    fetch(i).start()
            load_rows(near_ref, far_ref, rows_ref)
            if down is not None:
                out_refs[-1][...] = lax.dot_general(
                    rows_ref[...],
                    refs[len(inputs) - 1][0],
                    ROWS_BY_ROWS,
                    preferred_element_type=F32,
                )

        if tiles != "streamed":
            columns = pl.ds(pl.multiple_of(at * tile, tile), tile)
            put(
                at * tile,
                tile,
                jnp.dot(rows_ref[...], held_ref[:, columns], preferred_element_type=F32),
            )

        if tiles != "held":
            turn = at if tiles == "streamed" else at - 1

            @pl.when((turn >= 0) & (turn < pieces))
            def _():
                fetch(turn).wait()
                total = jnp.dot(
                    rows_ref[...], piece_ref[lax.rem(turn, slots)], preferred_element_type=F32
                )
                put(HELD * tile + turn * piece, piece, total)

                @pl.when(turn + slots < pieces)
                def _():
                    fetch(turn + slots).start()

    return pl.pallas_call(
        kernel,
        grid=(pieces if tiles == "streamed" else HELD,),
        in_specs=[VMEM] * (len(pair) + 1) + [ANY] + [VMEM] * (len(inputs) - len(pair) - 2),
        out_specs=[VMEM] * len(outputs),
        out_shape=outputs,
        scratch_shapes=[
            pltpu.VMEM((half, depth), BF16),
            pltpu.VMEM((slots, depth, piece), BF16),
            pltpu.SemaphoreType.DMA((slots,)),
        ],
        input_output_aliases={0: 0, 1: 1} if pair else {},
        compiler_params=params(14 if tiles == "streamed" else 10),
        name="base_chunk",
    )(*inputs)


def low_last(near, far, down, lows, levels):
    shard, depth = near.shape
    rank = down.shape[1]
    half = 2 * shard
    pairs = levels // 2

    def kernel(*refs):
        near_ref, far_ref, down_ref = refs[:3]
        low_refs = refs[3 : 2 + levels]
        keep_ref, send_ref, rows_ref = refs[2 + levels :]
        load_rows(near_ref, far_ref, rows_ref)
        last = lax.dot_general(
            rows_ref[...], down_ref[0], ROWS_BY_ROWS, preferred_element_type=F32
        )
        for k in range(pairs):
            rows = pair_rows(k, levels, half)
            first = low_refs[k][...]
            second = last if k == pairs - 1 else low_refs[k + pairs][...]
            mine = keeps_first(k, levels)
            keep_ref[rows, :] = jnp.where(mine, first, second)
            send_ref[rows, :] = jnp.where(mine, second, first)

    return pl.pallas_call(
        kernel,
        in_specs=[VMEM] * (2 + levels),
        out_specs=[VMEM] * 2,
        out_shape=[jax.ShapeDtypeStruct((pairs * half, rank), F32)] * 2,
        scratch_shapes=[pltpu.VMEM((half, depth), BF16)],
        compiler_params=params(6),
        name="low_last",
    )(near, far, down, *lows)


def low_own(keep, receive, store_row):
    def kernel(keep_ref, receive_ref, row_ref, out_ref):
        total = keep_ref[...] + receive_ref[...]
        out_ref[...] = jnp.where(row_ref[...] == lax.axis_index("mp"), total, 0.0).astype(BF16)

    return pl.pallas_call(
        kernel,
        in_specs=[VMEM] * 3,
        out_specs=VMEM,
        out_shape=jax.ShapeDtypeStruct(keep.shape, BF16),
        compiler_params=params(6),
        name="low_own",
    )(keep, receive, store_row)


def add(one, two):
    def kernel(one_ref, two_ref, out_ref):
        out_ref[...] = one_ref[...] + two_ref[...]

    return pl.pallas_call(
        kernel,
        in_specs=[VMEM] * 2,
        out_specs=VMEM,
        out_shape=jax.ShapeDtypeStruct(one.shape, one.dtype),
        compiler_params=params(6),
        name="add",
    )(one, two)


def finish(keeps, receives, lows, store_row, panels, offsets, levels):
    half, width = keeps[0].shape
    pairs = levels // 2
    total_rows, rank = lows[0].shape
    quarter = rank // 4
    parts = len(panels[0])
    blocks = len(offsets)
    tile = width // 2
    flat = [array for group in panels for array in group]

    def kernel(*refs):
        keep_refs, receive_refs = refs[:pairs], refs[pairs : 2 * pairs]
        row_ref = refs[2 * pairs]
        panel_refs = refs[2 * pairs + 1 : 2 * pairs + 1 + len(flat)]
        low_refs = refs[2 * pairs + 1 + len(flat) : -2]
        out_ref, spread_ref = refs[-2:]

        @pl.when(pl.program_id(0) == 0)
        def _():
            low = low_refs[0][...]
            for other in low_refs[1:]:
                low = low + other[...]
            group, core = lax.rem(lax.axis_index("groups"), 2), lax.axis_index("sub")
            z, y = position(levels)
            span = blocks * quarter
            at = lax.broadcasted_iota(jnp.int32, (rank, span), 0)
            to = lax.broadcasted_iota(jnp.int32, (rank, span), 1)
            block = lax.broadcasted_iota(jnp.int32, (total_rows, span), 1) // quarter
            row = jnp.zeros((total_rows, span), jnp.int32)
            for i, (dz, dy) in enumerate(offsets):
                source = 2 * lax.rem(z - dz + levels, levels) + (1 - y if dy else y)
                row = jnp.where(block == i, source, row)
            mine = row == row_ref[...]
            for i, (own_group, own_core) in enumerate(
                ((True, True), (False, True), (True, False), (False, False))
            ):
                which = 2 * (group if own_group else 1 - group) + (core if own_core else 1 - core)
                picks = (at == which * quarter + lax.rem(to, quarter)).astype(BF16)
                spread = jnp.dot(low, picks, preferred_element_type=F32)
                spread = jnp.where(mine, spread, 0.0).astype(BF16)
                spread_ref[:, i * span : (i + 1) * span] = spread

        panel = jnp.concatenate(
            [ref[...].reshape(ref.shape[0] * quarter, tile) for ref in panel_refs], axis=0
        )
        columns = pl.ds(pl.multiple_of(pl.program_id(0) * tile, tile), tile)
        for k in range(pairs):
            rows = pair_rows(k, levels, half)
            delta = jnp.dot(spread_ref[rows, :], panel, preferred_element_type=F32)
            base = keep_refs[k][:, columns] + receive_refs[k][...].astype(F32)
            out_ref[rows, :] = (base + delta).astype(BF16)

    column = lambda i: (0, i)
    return pl.pallas_call(
        kernel,
        grid=(width // tile,),
        in_specs=[VMEM] * pairs
        + [pl.BlockSpec((half, tile), column)] * pairs
        + [VMEM]
        + [pl.BlockSpec((array.shape[0], quarter, tile), lambda i: (0, 0, i)) for array in flat]
        + [VMEM] * len(lows),
        out_specs=pl.BlockSpec((total_rows, tile), column),
        out_shape=jax.ShapeDtypeStruct((total_rows, width), BF16),
        scratch_shapes=[pltpu.VMEM((total_rows, blocks * rank), BF16)],
        compiler_params=params(16),
        name="finish",
    )(*in_vmem(*keeps), *receives, store_row, *flat, *lows)


def swap(axis, size):
    def move(value):
        return lax.ppermute(value, axis, [(i, i ^ 1) for i in range(size)])

    return move


def per_device(tokens, gate, down, up, request_index, store_rows):
    count = store_rows.shape[0]
    levels = count // 2
    pairs = levels // 2
    shard = tokens.shape[0]
    own_tokens = shard * count // 2
    along_y = swap("mp", count)
    other_core = swap("sub", 2)
    other_group = swap("groups", lax.axis_size("groups"))
    together = lax.optimization_barrier
    down = jnp.swapaxes(down, 1, 2)

    def along_mp(value, dz, dy=0):
        pairs_of = [(i, 2 * ((i // 2 + dz) % levels) + ((i % 2) ^ dy)) for i in range(count)]
        return lax.ppermute(value, "mp", pairs_of)

    store_row = rows_of_tokens(request_index.reshape(1, -1), store_rows, own_tokens)

    early = [(1, 0), (0, 1)]
    crossing = [(dz, 1) for dz in range(1, levels) if dz != pairs]
    beside_last = [(dz, 0) for dz in range(2, levels)]
    late = [(pairs, 1)]
    first_offsets = [(0, 0)] + early + crossing
    second_offsets = beside_last + late
    offsets = first_offsets + second_offsets
    blocks = dict(zip(offsets, split_panels(up, offsets, levels)))

    def move_blocks(chosen):
        for dz, dy in chosen:
            if (dz, dy) != (0, 0):
                blocks[dz, dy] = along_mp(blocks[dz, dy], dz, dy)

    held, mark = hold_gate(gate)
    pair_left, lows, chunks = {}, [], []

    def multiply(k, near, far, down, after=None, tiles="all"):
        pair = pair_left.get(k % pairs, ())
        made = base_chunk(near, far, gate, held, pair, down, k, levels, after, tiles)
        pair_left[k % pairs] = made[:2]
        if down is not None:
            lows.append(made[-1])

    near = tokens
    for stage in range(levels):
        far = along_y(near)
        after = along_mp(near, 1) if stage < levels - 1 else near
        if stage == 0:
            move_blocks(early)
            bound = [store_row, mark]
        else:
            multiply(stage - 1, *chunks[-1], down, mark if stage == 1 else None)
            bound = [lows[-1]]
        if stage == levels - 1:
            first_x, first_c = other_group(first), other_core(first)
            move_blocks(beside_last)
        elif stage > 0:
            move_blocks(crossing[stage - 1 : stage])
        names = list(blocks)
        near, after, far, moved, bound = together(
            (near, after, far, [blocks[name] for name in names], bound)
        )
        blocks = dict(zip(names, moved))
        if stage == 0:
            store_row, mark = bound
        else:
            lows[-1] = bound[0]
        if stage == levels - 2:
            first = stack([blocks[offset] for offset in first_offsets])
        chunks.append((near, far))
        near = after

    near, far = chunks[-1]
    last = levels - 1
    move_blocks(late)
    low_keep, low_send = low_last(near, far, down, lows, levels)
    low_send, first_x = together((low_send, first_x))
    first_xc = other_core(first_x)
    low = low_own(low_keep, other_core(low_send), store_row)

    crossed = along_y(low)
    multiply(last, near, far, None, tiles="held")
    moved = [blocks[offset] for offset in second_offsets]
    low, crossed, pair_left[last % pairs], moved, first, first_xc, first_c = together(
        (low, crossed, pair_left[last % pairs], moved, first, first_xc, first_c)
    )
    second = stack(moved)
    second_x, second_c = other_group(second), other_core(second)
    low = add(low, crossed)
    parts = [along_mp(low, j) for j in range(1, levels)]
    multiply(last, near, far, None, tiles="streamed")
    low, parts, pair_left[last % pairs], second_x, second_c = together(
        (low, parts, pair_left[last % pairs], second_x, second_c)
    )
    parts = [low] + parts
    receives = [other_core(pair_left[k][1]) for k in range(pairs)]
    keeps = [pair_left[k][0] for k in range(pairs)]
    panels = [
        (first, second),
        (first_x, second_x),
        (first_c, second_c),
        (first_xc, other_core(second_x)),
    ]
    return finish(keeps, receives, parts, store_row, panels, offsets, levels)


def solution(mesh):
    return jax.shard_map(
        per_device,
        mesh=mesh,
        in_specs=(
            P(("groups", "mp"), "sub"),
            P("sub", "mp"),
            P("mp", "sub", None),
            P("mp", None, None),
            P("groups", None),
            P(),
        ),
        out_specs=P(("groups", "sub"), "mp"),
        check_vma=False,
    )
```

```python
import jax
import jax.numpy as jnp
from jax import lax
from jax.experimental import pallas as pl
from jax.experimental.pallas import tpu as pltpu
from jax.sharding import PartitionSpec as P

F32 = jnp.float32
BF16 = jnp.bfloat16
ANY = pl.BlockSpec(memory_space=pl.ANY)
VMEM = pl.BlockSpec(memory_space=pltpu.VMEM)
ROWS_BY_ROWS = (((1,), (1,)), ((), ()))


def in_vmem(*values):
    return [pltpu.with_memory_space_constraint(value, pltpu.VMEM) for value in values]


def params(mib):
    return pltpu.CompilerParams(vmem_limit_bytes=mib << 20)


def run_copies(copies):
    for copy in copies:
        copy.start()
    for copy in copies:
        copy.wait()


def in_hbm(*values):
    return [pltpu.with_memory_space_constraint(value, pltpu.HBM) for value in values]


def position(levels):
    index = lax.axis_index("mp")
    return index // 2, lax.rem(index, 2)


def rows_of_tokens(requests, store_rows, tokens):
    count = requests.shape[1]

    def kernel(requests_ref, rows_ref, out_ref):
        request = requests_ref[...]
        row = jnp.zeros_like(request)
        for i in range(store_rows.shape[0]):
            row = jnp.where(request == i, rows_ref[i], row)
        token = lax.axis_index("sub") * tokens + lax.broadcasted_iota(
            jnp.int32, (tokens, count), 0
        )
        own = token // 2 == lax.broadcasted_iota(jnp.int32, (tokens, count), 1)
        chosen = jnp.where(own, row.astype(F32), 0.0)
        out_ref[...] = jnp.sum(chosen, axis=1, keepdims=True).astype(jnp.int32)

    return pl.pallas_call(
        kernel,
        in_specs=[VMEM, pl.BlockSpec(memory_space=pltpu.SMEM)],
        out_specs=VMEM,
        out_shape=jax.ShapeDtypeStruct((tokens, 1), jnp.int32),
        compiler_params=params(6),
        name="rows_of_tokens",
    )(requests, store_rows)


def split_panels(up, offsets, levels):
    rank, hidden = up.shape[1], up.shape[2]
    quarter, width = rank // 4, hidden // (2 * levels)

    def kernel(up_ref, *refs):
        out_refs, sem = refs[:-1], refs[-1]
        z, y = position(levels)
        which = 2 * lax.rem(lax.axis_index("groups"), 2) + lax.axis_index("sub")
        rows = pl.ds(pl.multiple_of(which * quarter, quarter), quarter)
        copies = []
        for i, (dz, dy) in enumerate(offsets):
            to = 2 * lax.rem(z + dz, levels) + (1 - y if dy else y)
            columns = pl.ds(pl.multiple_of(to * width, 128), width)
            copies.append(
                pltpu.make_async_copy(up_ref.at[0, rows, columns], out_refs[i], sem.at[i])
            )
        run_copies(copies)

    return pl.pallas_call(
        kernel,
        in_specs=[ANY],
        out_specs=[VMEM] * len(offsets),
        out_shape=[jax.ShapeDtypeStruct((quarter, width), BF16)] * len(offsets),
        scratch_shapes=[pltpu.SemaphoreType.DMA((len(offsets),))],
        compiler_params=params(6),
        name="split_panels",
    )(*in_hbm(up))


def stack(blocks):
    count = len(blocks)

    def kernel(*refs):
        run_copies(
            [pltpu.make_async_copy(refs[i], refs[count].at[i], refs[-1].at[i]) for i in range(count)]
        )

    return pl.pallas_call(
        kernel,
        in_specs=[ANY] * count,
        out_specs=VMEM,
        out_shape=jax.ShapeDtypeStruct((count, *blocks[0].shape), BF16),
        scratch_shapes=[pltpu.SemaphoreType.DMA((count,))],
        compiler_params=params(6),
        name="stack",
    )(*blocks)


HELD, PARTS = 5, 7


def hold_gate(gate):
    depth, width = gate.shape
    columns = width // PARTS * HELD
    pieces = 8

    def kernel(gate_ref, out_ref, mark_ref, sem):
        mark_ref[...] = jnp.zeros_like(mark_ref)
        size = depth // pieces
        run_copies(
            [
                pltpu.make_async_copy(
                    gate_ref.at[pl.ds(i * size, size), pl.ds(0, columns)],
                    out_ref.at[pl.ds(i * size, size)],
                    sem.at[i],
                )
                for i in range(pieces)
            ]
        )

    return pl.pallas_call(
        kernel,
        in_specs=[ANY],
        out_specs=[VMEM, VMEM],
        out_shape=[pltpu.VMEM((depth, columns), BF16), jax.ShapeDtypeStruct((8, 128), F32)],
        scratch_shapes=[pltpu.SemaphoreType.DMA((pieces,))],
        compiler_params=params(6),
        name="hold_gate",
    )(gate)


def keeps_first(step, levels):
    origin = lax.rem(position(levels)[0] - step + levels, levels)
    return (origin // (levels // 2)) == lax.axis_index("sub")


def pair_rows(step, levels, half):
    at = lax.rem(position(levels)[0] - step + levels, levels // 2)
    return pl.ds(pl.multiple_of(at * half, half), half)


def load_rows(near_ref, far_ref, rows_ref):
    shard = near_ref.shape[0]
    y = position(2)[1]
    rows_ref[pl.ds(pl.multiple_of(y * shard, shard), shard), :] = near_ref[...]
    rows_ref[pl.ds(pl.multiple_of((1 - y) * shard, shard), shard), :] = far_ref[...]


def base_chunk(near, far, gate, held, pair, down, step, levels, after=None, tiles="all"):
    shard, depth = near.shape
    width = gate.shape[1]
    tile = width // PARTS
    piece = tile // 2
    pieces = 2 * (PARTS - HELD)
    assert pieces < HELD
    slots = pieces if tiles == "streamed" else 2
    half = 2 * shard
    inputs = in_vmem(*pair, held) + [gate, near, far]
    outputs = [pltpu.VMEM((half, width), F32), pltpu.VMEM((half, width), BF16)]
    if after is not None:
        inputs.append(after)
    if down is not None:
        inputs.append(down)
        outputs.append(jax.ShapeDtypeStruct((half, down.shape[1]), F32))

    def kernel(*refs):
        held_ref, gate_ref, near_ref, far_ref = refs[len(pair) : len(pair) + 4]
        out_refs, (rows_ref, piece_ref, sem) = refs[len(inputs) : -3], refs[-3:]
        mine = keeps_first(step, levels)
        at = pl.program_id(0)

        def fetch(i):
            begin = pl.multiple_of(HELD * tile + i * piece, piece)
            slot = lax.rem(i, slots)
            return pltpu.make_async_copy(
                gate_ref.at[:, pl.ds(begin, piece)], piece_ref.at[slot], sem.at[slot]
            )

        def put(begin, size, total):
            columns = pl.ds(pl.multiple_of(begin, size), size)

            @pl.when(mine)
            def _():
                out_refs[0][:, columns] = total

            @pl.when(jnp.logical_not(mine))
            def _():
                out_refs[1][:, columns] = total.astype(BF16)

        @pl.when(at == 0)
        def _():
            if tiles != "held":
                for i in range(slots):
                    fetch(i).start()
            load_rows(near_ref, far_ref, rows_ref)
            if down is not None:
                out_refs[-1][...] = lax.dot_general(
                    rows_ref[...],
                    refs[len(inputs) - 1][0],
                    ROWS_BY_ROWS,
                    preferred_element_type=F32,
                )

        if tiles != "streamed":
            columns = pl.ds(pl.multiple_of(at * tile, tile), tile)
            put(
                at * tile,
                tile,
                jnp.dot(rows_ref[...], held_ref[:, columns], preferred_element_type=F32),
            )

        if tiles != "held":
            turn = at if tiles == "streamed" else at - 1

            @pl.when((turn >= 0) & (turn < pieces))
            def _():
                fetch(turn).wait()
                total = jnp.dot(
                    rows_ref[...], piece_ref[lax.rem(turn, slots)], preferred_element_type=F32
                )
                put(HELD * tile + turn * piece, piece, total)

                @pl.when(turn + slots < pieces)
                def _():
                    fetch(turn + slots).start()

    return pl.pallas_call(
        kernel,
        grid=(pieces if tiles == "streamed" else HELD,),
        in_specs=[VMEM] * (len(pair) + 1) + [ANY] + [VMEM] * (len(inputs) - len(pair) - 2),
        out_specs=[VMEM] * len(outputs),
        out_shape=outputs,
        scratch_shapes=[
            pltpu.VMEM((half, depth), BF16),
            pltpu.VMEM((slots, depth, piece), BF16),
            pltpu.SemaphoreType.DMA((slots,)),
        ],
        input_output_aliases={0: 0, 1: 1} if pair else {},
        compiler_params=params(14 if tiles == "streamed" else 10),
        name="base_chunk",
    )(*inputs)


def low_last(near, far, down, lows, levels):
    shard, depth = near.shape
    rank = down.shape[1]
    half = 2 * shard
    pairs = levels // 2

    def kernel(*refs):
        near_ref, far_ref, down_ref = refs[:3]
        low_refs = refs[3 : 2 + levels]
        keep_ref, send_ref, rows_ref = refs[2 + levels :]
        load_rows(near_ref, far_ref, rows_ref)
        last = lax.dot_general(
            rows_ref[...], down_ref[0], ROWS_BY_ROWS, preferred_element_type=F32
        )
        for k in range(pairs):
            rows = pair_rows(k, levels, half)
            first = low_refs[k][...]
            second = last if k == pairs - 1 else low_refs[k + pairs][...]
            mine = keeps_first(k, levels)
            keep_ref[rows, :] = jnp.where(mine, first, second)
            send_ref[rows, :] = jnp.where(mine, second, first)

    return pl.pallas_call(
        kernel,
        in_specs=[VMEM] * (2 + levels),
        out_specs=[VMEM] * 2,
        out_shape=[jax.ShapeDtypeStruct((pairs * half, rank), F32)] * 2,
        scratch_shapes=[pltpu.VMEM((half, depth), BF16)],
        compiler_params=params(6),
        name="low_last",
    )(near, far, down, *lows)


def low_own(keep, receive, store_row):
    def kernel(keep_ref, receive_ref, row_ref, out_ref):
        total = keep_ref[...] + receive_ref[...]
        out_ref[...] = jnp.where(row_ref[...] == lax.axis_index("mp"), total, 0.0).astype(BF16)

    return pl.pallas_call(
        kernel,
        in_specs=[VMEM] * 3,
        out_specs=VMEM,
        out_shape=jax.ShapeDtypeStruct(keep.shape, BF16),
        compiler_params=params(6),
        name="low_own",
    )(keep, receive, store_row)


def add(one, two):
    def kernel(one_ref, two_ref, out_ref):
        out_ref[...] = one_ref[...] + two_ref[...]

    return pl.pallas_call(
        kernel,
        in_specs=[VMEM] * 2,
        out_specs=VMEM,
        out_shape=jax.ShapeDtypeStruct(one.shape, one.dtype),
        compiler_params=params(6),
        name="add",
    )(one, two)


def finish(keeps, receives, lows, store_row, panels, offsets, levels):
    half, width = keeps[0].shape
    pairs = levels // 2
    total_rows, rank = lows[0].shape
    quarter = rank // 4
    parts = len(panels[0])
    blocks = len(offsets)
    tile = width // 2
    flat = [array for group in panels for array in group]

    def kernel(*refs):
        keep_refs, receive_refs = refs[:pairs], refs[pairs : 2 * pairs]
        row_ref = refs[2 * pairs]
        panel_refs = refs[2 * pairs + 1 : 2 * pairs + 1 + len(flat)]
        low_refs = refs[2 * pairs + 1 + len(flat) : -2]
        out_ref, spread_ref = refs[-2:]

        @pl.when(pl.program_id(0) == 0)
        def _():
            low = low_refs[0][...]
            for other in low_refs[1:]:
                low = low + other[...]
            group, core = lax.rem(lax.axis_index("groups"), 2), lax.axis_index("sub")
            z, y = position(levels)
            span = blocks * quarter
            at = lax.broadcasted_iota(jnp.int32, (rank, span), 0)
            to = lax.broadcasted_iota(jnp.int32, (rank, span), 1)
            block = lax.broadcasted_iota(jnp.int32, (total_rows, span), 1) // quarter
            row = jnp.zeros((total_rows, span), jnp.int32)
            for i, (dz, dy) in enumerate(offsets):
                source = 2 * lax.rem(z - dz + levels, levels) + (1 - y if dy else y)
                row = jnp.where(block == i, source, row)
            mine = row == row_ref[...]
            for i, (own_group, own_core) in enumerate(
                ((True, True), (False, True), (True, False), (False, False))
            ):
                which = 2 * (group if own_group else 1 - group) + (core if own_core else 1 - core)
                picks = (at == which * quarter + lax.rem(to, quarter)).astype(BF16)
                spread = jnp.dot(low, picks, preferred_element_type=F32)
                spread = jnp.where(mine, spread, 0.0).astype(BF16)
                spread_ref[:, i * span : (i + 1) * span] = spread

        panel = jnp.concatenate(
            [ref[...].reshape(ref.shape[0] * quarter, tile) for ref in panel_refs], axis=0
        )
        columns = pl.ds(pl.multiple_of(pl.program_id(0) * tile, tile), tile)
        for k in range(pairs):
            rows = pair_rows(k, levels, half)
            delta = jnp.dot(spread_ref[rows, :], panel, preferred_element_type=F32)
            base = keep_refs[k][:, columns] + receive_refs[k][...].astype(F32)
            out_ref[rows, :] = (base + delta).astype(BF16)

    column = lambda i: (0, i)
    return pl.pallas_call(
        kernel,
        grid=(width // tile,),
        in_specs=[VMEM] * pairs
        + [pl.BlockSpec((half, tile), column)] * pairs
        + [VMEM]
        + [pl.BlockSpec((array.shape[0], quarter, tile), lambda i: (0, 0, i)) for array in flat]
        + [VMEM] * len(lows),
        out_specs=pl.BlockSpec((total_rows, tile), column),
        out_shape=jax.ShapeDtypeStruct((total_rows, width), BF16),
        scratch_shapes=[pltpu.VMEM((total_rows, blocks * rank), BF16)],
        compiler_params=params(16),
        name="finish",
    )(*in_vmem(*keeps), *receives, store_row, *flat, *lows)


def swap(axis, size):
    def move(value):
        return lax.ppermute(value, axis, [(i, i ^ 1) for i in range(size)])

    return move


def per_device(tokens, gate, down, up, request_index, store_rows):
    count = store_rows.shape[0]
    levels = count // 2
    pairs = levels // 2
    shard = tokens.shape[0]
    own_tokens = shard * count // 2
    along_y = swap("mp", count)
    other_core = swap("sub", 2)
    other_group = swap("groups", lax.axis_size("groups"))
    together = lax.optimization_barrier
    down = jnp.swapaxes(down, 1, 2)

    def along_mp(value, dz, dy=0):
        pairs_of = [(i, 2 * ((i // 2 + dz) % levels) + ((i % 2) ^ dy)) for i in range(count)]
        return lax.ppermute(value, "mp", pairs_of)

    store_row = rows_of_tokens(request_index.reshape(1, -1), store_rows, own_tokens)

    early = [(1, 0), (0, 1)]
    crossing = [(dz, 1) for dz in range(1, levels) if dz != pairs]
    beside_last = [(dz, 0) for dz in range(2, levels)]
    late = [(pairs, 1)]
    first_offsets = [(0, 0)] + early + crossing
    second_offsets = beside_last + late
    offsets = first_offsets + second_offsets
    blocks = dict(zip(offsets, split_panels(up, offsets, levels)))

    def move_blocks(chosen):
        for dz, dy in chosen:
            if (dz, dy) != (0, 0):
                blocks[dz, dy] = along_mp(blocks[dz, dy], dz, dy)

    held, mark = hold_gate(gate)
    pair_left, lows, chunks = {}, [], []

    def multiply(k, near, far, down, after=None, tiles="all"):
        pair = pair_left.get(k % pairs, ())
        made = base_chunk(near, far, gate, held, pair, down, k, levels, after, tiles)
        pair_left[k % pairs] = made[:2]
        if down is not None:
            lows.append(made[-1])

    near = tokens
    for stage in range(levels):
        after = along_mp(near, 1) if stage < levels - 1 else near
        far = along_y(near)
        if stage == 0:
            move_blocks(early)
            bound = [store_row, mark]
        else:
            multiply(stage - 1, *chunks[-1], down, mark if stage == 1 else None)
            bound = [lows[-1]]
        if stage == levels - 1:
            first_x, first_c = other_group(first), other_core(first)
            move_blocks(beside_last)
        elif stage > 0:
            move_blocks(crossing[stage - 1 : stage])
        names = list(blocks)
        near, after, far, moved, bound = together(
            (near, after, far, [blocks[name] for name in names], bound)
        )
        blocks = dict(zip(names, moved))
        if stage == 0:
            store_row, mark = bound
        else:
            lows[-1] = bound[0]
        if stage == levels - 2:
            first = stack([blocks[offset] for offset in first_offsets])
        chunks.append((near, far))
        near = after

    near, far = chunks[-1]
    last = levels - 1
    move_blocks(late)
    low_keep, low_send = low_last(near, far, down, lows, levels)
    low_send, first_x = together((low_send, first_x))
    first_xc = other_core(first_x)
    low = low_own(low_keep, other_core(low_send), store_row)

    crossed = along_y(low)
    multiply(last, near, far, None, tiles="held")
    moved = [blocks[offset] for offset in second_offsets]
    low, crossed, pair_left[last % pairs], moved, first, first_xc, first_c = together(
        (low, crossed, pair_left[last % pairs], moved, first, first_xc, first_c)
    )
    second = stack(moved)
    second_x, second_c = other_group(second), other_core(second)
    low = add(low, crossed)
    parts = [along_mp(low, j) for j in range(1, levels)]
    multiply(last, near, far, None, tiles="streamed")
    low, parts, pair_left[last % pairs], second_x, second_c = together(
        (low, parts, pair_left[last % pairs], second_x, second_c)
    )
    parts = [low] + parts
    receives = [other_core(pair_left[k][1]) for k in range(pairs)]
    keeps = [pair_left[k][0] for k in range(pairs)]
    panels = [
        (first, second),
        (first_x, second_x),
        (first_c, second_c),
        (first_xc, other_core(second_x)),
    ]
    return finish(keeps, receives, parts, store_row, panels, offsets, levels)


def solution(mesh):
    return jax.shard_map(
        per_device,
        mesh=mesh,
        in_specs=(
            P(("groups", "mp"), "sub"),
            P("sub", "mp"),
            P("mp", "sub", None),
            P("mp", None, None),
            P("groups", None),
            P(),
        ),
        out_specs=P(("groups", "sub"), "mp"),
        check_vma=False,
    )
```
